32 devices in a mesh: section: 2 (over x), tensor: 4 (over z), dp: 4 (over y, core).
Axes of the slice: x: 2, y: 2, z: 4, core: 2. Of those that a mesh axis runs over, the one named last changes fastest.
Arguments:
- boundary: bfloat16 [2, 4, 8, 1024, 1024], P('section', None, 'dp', 'tensor'), may hold values from -6 to 6
- counts: int32 [4, 4], P(None, 'dp'), may hold values from 1 to 2, as said below
- attend_gain: float32 [2, 1024], P('section'), may hold values from 0.5 to 1.5
- attend_shift: float32 [2, 1024], P('section'), may hold values from -1.75 to 1.75
- triple_weight: bfloat16 [2, 1024, 3, 1024], P('section', None, None, 'tensor'), may hold values from -0.1875 to 0.1875
- triple_bias: float32 [2, 2, 1024], P('section', None, 'tensor'), may hold values from -3 to 3
- merge_weight: bfloat16 [2, 1024, 1024], P('section', 'tensor'), may hold values from -0.75 to 0.75
- merge_bias: float32 [2, 1024], P('section'), may hold values from -1.75 to 1.75
- attend_scale: float32 [2, 1024], P('section'), may hold values from 0.3 to 1
- feed_gain: float32 [2, 1024], P('section'), may hold values from 0.5 to 1.5
- feed_shift: float32 [2, 1024], P('section'), may hold values from -1.75 to 1.75
- expand_weight: bfloat16 [2, 1024, 4096], P('section', None, 'tensor'), may hold values from -0.1875 to 0.1875
- expand_bias: float32 [2, 4096], P('section', 'tensor'), may hold values from -3 to 3
- shrink_weight: bfloat16 [2, 4096, 1024], P('section', 'tensor'), may hold values from -0.09375 to 0.09375
- shrink_bias: float32 [2, 1024], P('section'), may hold values from -1.75 to 1.75
- feed_scale: float32 [2, 1024], P('section'), may hold values from 0.3 to 1
Outputs:
- boundary_grad: bfloat16 [2, 4, 8, 1024, 1024], P('section', None, 'dp', 'tensor')
- attend_gain_grad: float32 [2, 1024], P('section')
- attend_shift_grad: float32 [2, 1024], P('section')
- triple_weight_grad: float32 [2, 1024, 3, 1024], P('section', None, None, 'tensor')
- triple_bias_grad: float32 [2, 2, 1024], P('section', None, 'tensor')
- merge_weight_grad: float32 [2, 1024, 1024], P('section', 'tensor')
- merge_bias_grad: float32 [2, 1024], P('section')
- attend_scale_grad: float32 [2, 1024], P('section')
- feed_gain_grad: float32 [2, 1024], P('section')
- feed_shift_grad: float32 [2, 1024], P('section')
- expand_weight_grad: float32 [2, 1024, 4096], P('section', None, 'tensor')
- expand_bias_grad: float32 [2, 4096], P('section', 'tensor')
- shrink_weight_grad: float32 [2, 4096, 1024], P('section', 'tensor')
- shrink_bias_grad: float32 [2, 1024], P('section')
- feed_scale_grad: float32 [2, 1024], P('section')
The draws below stay inside these ranges and needn't reach their ends.
Inputs may be any that keep to these rules, and one draw needn't show every extreme that they name: Replica r holds images in its slots 0 to counts[m, r] - 1 of micro-batch m; in every micro-batch one replica holds 2 and another holds 1.
All inputs are finite; a program needn't handle non-finite values.
Results may differ from the reference program's by a relative error of at most 0.02.
Values may be sent and summed in bfloat16 or wider, within the bound.
No kernel may reach another device: no remote copies, remote signals or barrier semaphores. Data moves between devices by JAX's collectives and lax.ppermute only.
A program may use at most 640 MiB of HBM per device.

```python
import math
import jax
import jax.numpy as jnp
from jax import lax

D = 1024
HEADS = 16
HD = 64
FF = 4096
SEQ = 1024
CAP = 2
MICRO = 4
SLOTS = 8
N_DP = 4


def draw_counts(key, part):
    key = jax.random.fold_in(key, 7)
    first_key, second_key, third_key = jax.random.split(key, 3)
    base_counts = jax.random.randint(first_key, (MICRO, N_DP), 1, CAP + 1)
    fullest = jax.random.randint(second_key, (MICRO, 1), 0, N_DP)
    step_away = jax.random.randint(third_key, (MICRO, 1), 1, N_DP)
    emptiest = (fullest + step_away) % N_DP
    column = lax.broadcasted_iota(jnp.int32, (MICRO, N_DP), 1)
    shaped = jnp.where(column == emptiest, 1, base_counts)
    return jnp.where(column == fullest, CAP, shaped).astype(jnp.int32)


def levels(key, extent, cuts, smallest, high):
    level = 1.0
    for axis_at, blocks in cuts:
        draws = jax.random.uniform(jax.random.fold_in(jax.random.fold_in(key, 6), axis_at), (blocks,), jnp.float32, smallest / len(cuts), high / len(cuts))
        level = level * jnp.repeat(jnp.exp(draws), extent[axis_at] // blocks).reshape((-1,) + (1,) * (len(extent) - 1 - axis_at))
    return level


def normal_values(rng, extent, width, most, cuts=(), kind=jnp.bfloat16):
    values = width * jax.random.normal(rng, extent, jnp.float32)
    if cuts:
        values = values * levels(rng, extent, cuts, -0.22, 0.18)
    return jnp.clip(values, -most, most).astype(kind)


def setup_inputs(seed: int = 0) -> dict:
    key_of = jax.random.split(jax.random.key(seed), 17)
    boundary = normal_values(key_of[0], (2, MICRO, SLOTS, SEQ, D), 1.0, 6.0, ((0, 2), (2, 4), (3, 4)))
    counts = draw_counts(jax.random.fold_in(key_of[16], 71), 0)
    attend_gain = jnp.clip(1.0 + 0.1 * jax.random.normal(key_of[2], (2, D), jnp.float32), 0.5, 1.5)
    attend_shift = normal_values(key_of[3], (2, D), 0.3, 1.75, ((0, 2),), jnp.float32)
    triple_weight = normal_values(key_of[4], (2, D, 3, D), D ** -0.5, 0.1875, ((0, 2), (3, 4)))
    triple_bias = normal_values(key_of[5], (2, 2, D), 0.5, 3.0, ((0, 2), (2, 4)), jnp.float32)
    merge_weight = normal_values(key_of[6], (2, D, D), (D // 16) ** -0.5, 0.75, ((0, 2), (1, 4)))
    merge_bias = normal_values(key_of[7], (2, D), 0.3, 1.75, ((0, 2),), jnp.float32)
    attend_scale = jnp.clip(jnp.exp(math.log(1.0) - 1.2039728 * jax.random.uniform(key_of[8], (2, D), jnp.float32) ** levels(key_of[8], (2, D), ((0, 2),), -0.2, 0.2)), 0.3, 1.0)
    feed_gain = jnp.clip(1.0 + 0.1 * jax.random.normal(key_of[9], (2, D), jnp.float32), 0.5, 1.5)
    feed_shift = normal_values(key_of[10], (2, D), 0.3, 1.75, ((0, 2),), jnp.float32)
    expand_weight = normal_values(key_of[11], (2, D, FF), D ** -0.5, 0.1875, ((0, 2), (2, 4)))
    expand_bias = normal_values(key_of[12], (2, FF), 0.5, 3.0, ((0, 2), (1, 4)), jnp.float32)
    shrink_weight = normal_values(key_of[13], (2, FF, D), FF ** -0.5, 0.09375, ((0, 2), (1, 4)))
    shrink_bias = normal_values(key_of[14], (2, D), 0.3, 1.75, ((0, 2),), jnp.float32)
    feed_scale = jnp.clip(jnp.exp(math.log(1.0) - 1.2039728 * jax.random.uniform(key_of[15], (2, D), jnp.float32) ** levels(key_of[15], (2, D), ((0, 2),), -0.2, 0.2)), 0.3, 1.0)
    return {"boundary": boundary, "counts": counts, "attend_gain": attend_gain, "attend_shift": attend_shift, "triple_weight": triple_weight, "triple_bias": triple_bias, "merge_weight": merge_weight, "merge_bias": merge_bias, "attend_scale": attend_scale, "feed_gain": feed_gain, "feed_shift": feed_shift, "expand_weight": expand_weight, "expand_bias": expand_bias, "shrink_weight": shrink_weight, "shrink_bias": shrink_bias, "feed_scale": feed_scale}


epsilon = 1e-06
highest = lax.Precision.HIGHEST

@jax.custom_vjp
def low(v):
    return lax.optimization_barrier(v.astype(jnp.bfloat16)).astype(jnp.float32)

@jax.custom_vjp
def low_back(v):
    return v

def low_keep(v):
    return (low(v), None)

def low_pass(kept, grad):
    return (grad,)

def back_keep(v):
    return (v, None)

def back_low(kept, grad):
    return (low(grad),)
low.defvjp(low_keep, low_pass)
low_back.defvjp(back_keep, back_low)

def normalize(resid, gain, shift):
    centre = resid - lax.optimization_barrier(jnp.mean(resid, axis=-1, keepdims=True))
    spread = lax.optimization_barrier(jnp.mean(centre * centre, axis=-1, keepdims=True))
    return centre * lax.rsqrt(spread + epsilon) * gain + shift

def softmax_rows(scores):
    shifted = scores - lax.optimization_barrier(jnp.max(scores, axis=-1, keepdims=True))
    raised = jnp.exp(shifted)
    return raised / lax.optimization_barrier(jnp.sum(raised, axis=-1, keepdims=True))

def attend(queries, key_rows, value_rows):
    images, length = (queries.shape[0], queries.shape[1])
    block_rows = min(512, length)
    number = length // block_rows
    factor = HD ** (-0.5)
    blocks = queries.reshape(images, number, block_rows, HEADS, HD).transpose(1, 0, 2, 3, 4)

    def one_block(query_part):
        raw_scores = low_back(jnp.einsum('gqhe,gkhe->ghqk', query_part, key_rows, precision=highest))
        probability = low(softmax_rows(raw_scores * factor))
        return jnp.einsum('ghqk,gkhe->gqhe', probability, value_rows, precision=highest)
    pieces = lax.map(jax.checkpoint(one_block), blocks)
    return pieces.transpose(1, 0, 2, 3, 4).reshape(images, length, HEADS * HD)

def layer(resid, params):
    attend_gain, attend_shift, triple_weight, triple_bias, merge_weight, merge_bias, attend_scale, feed_gain, feed_shift, expand_weight, expand_bias, shrink_weight, shrink_bias, feed_scale = params
    images, length = (resid.shape[0], resid.shape[1])
    normed_one = low(normalize(resid, attend_gain, attend_shift))
    bias_full = jnp.stack([triple_bias[0], jnp.zeros_like(triple_bias[0]), triple_bias[1]])
    projected = jnp.einsum('gsd,dcf->gscf', normed_one, triple_weight, precision=highest) + bias_full
    projected = low(low_back(projected))
    split = projected.reshape(images, length, 3, HEADS, HD)
    attended = attend(split[:, :, 0], split[:, :, 1], split[:, :, 2])
    attended = low(low_back(attended))
    merged = low_back(jnp.einsum('gsf,fd->gsd', attended, merge_weight, precision=highest) + merge_bias)
    middle = resid + attend_scale * merged
    normed_two = low(normalize(middle, feed_gain, feed_shift))
    before = low_back(jnp.einsum('gsd,df->gsf', normed_two, expand_weight, precision=highest) + expand_bias)
    activated = low(jax.nn.gelu(before, approximate=False))
    shrunk = low_back(jnp.einsum('gsf,fd->gsd', activated, shrink_weight, precision=highest) + shrink_bias)
    return middle + feed_scale * shrunk

def reference(boundary, counts, attend_gain, attend_shift, triple_weight, triple_bias, merge_weight, merge_bias, attend_scale, feed_gain, feed_shift, expand_weight, expand_bias, shrink_weight, shrink_bias, feed_scale):
    params = tuple((weight.astype(jnp.float32) for weight in (attend_gain, attend_shift, triple_weight, triple_bias, merge_weight, merge_bias, attend_scale, feed_gain, feed_shift, expand_weight, expand_bias, shrink_weight, shrink_bias, feed_scale)))
    inputs = boundary[0].astype(jnp.float32).reshape(MICRO * N_DP, CAP, SEQ, D)
    live_slots = (lax.broadcasted_iota(jnp.int32, (MICRO, N_DP, CAP), 2) < counts[:, :, None]).astype(jnp.float32)
    cotangent = boundary[1].astype(jnp.float32).reshape(MICRO * N_DP, CAP, SEQ, D)
    cotangent = cotangent * live_slots.reshape(MICRO * N_DP, CAP, 1, 1)
    bumps = jnp.zeros_like(inputs)

    def whole(inputs, bumps, params):
        first_params = tuple((weight[0] for weight in params))
        second_params = tuple((weight[1] for weight in params))

        def group(carry, paired):
            images, extra = paired
            middle = low_back(low(layer(images, first_params)) + extra)
            return (carry, layer(middle, second_params))
        _, outputs = lax.scan(jax.checkpoint(group), jnp.zeros((), jnp.float32), (inputs, bumps))
        return outputs
    _, pullback = jax.vjp(whole, inputs, bumps, params)
    input_grad, middle_grad, param_grads = pullback(cotangent)
    boundary_grad = jnp.stack([input_grad, middle_grad]).reshape(2, MICRO, N_DP * CAP, SEQ, D).astype(jnp.bfloat16)
    return (boundary_grad, param_grads[0], param_grads[1], param_grads[2], param_grads[3], param_grads[4], param_grads[5], param_grads[6], param_grads[7], param_grads[8], param_grads[9], param_grads[10], param_grads[11], param_grads[12], param_grads[13])
```

```python
import functools
import math

import jax
import jax.numpy as jnp
from jax import lax
from jax.experimental import pallas as pl
from jax.experimental.pallas import tpu as pltpu
from jax.sharding import PartitionSpec as P

HD = 64
PAIR = 2 * HD

epsilon = 1e-06
inv_root_two = 1.0 / math.sqrt(2.0)
inv_root_tau = 1.0 / math.sqrt(2.0 * math.pi)
log2_e = math.log2(math.e)
score_scale = HD**-0.5

EVERY = ("section", "tensor", "dp")
GROUP = ("section", "tensor")
NN = (((1,), (0,)), ((), ()))
NT = (((1,), (1,)), ((), ()))
TN = (((0,), (0,)), ((), ()))
VMEM_LIMIT = 56 << 20
bf16 = jnp.bfloat16
f32 = jnp.float32


def mm(a, b, dims=NN):
    return lax.dot_general(a, b, dims, preferred_element_type=f32)


def attend_ahead_kernel(q_ref, k_ref, v_ref, out_ref, log_ref, *, block):
    length = q_ref.shape[0]
    lane = lax.broadcasted_iota(jnp.int32, (1, PAIR), 1)
    keys = k_ref[...]
    values = v_ref[...]
    padded = [jnp.where((lane // HD) == h, values, jnp.ones_like(values)) for h in range(2)]
    factor = log2_e * score_scale
    for start in range(0, length, block):
        rows = pl.ds(start, block)
        queries = q_ref[rows, :]
        pieces = []
        for h in range(2):
            own = jnp.where((lane // HD) == h, queries, jnp.zeros_like(queries))
            scores = mm(own, keys, NT)
            top = jnp.max(scores, axis=1, keepdims=True) * factor
            raised = jnp.exp2(scores * factor - top).astype(bf16)
            summed = mm(raised, padded[h])
            total = summed[:, (1 - h) * HD : (1 - h) * HD + 1]
            pieces.append(summed / total)
            column = jnp.broadcast_to(top + jnp.log2(total), (block, PAIR))
            log_ref[0, h, rows] = jnp.transpose(column)[0]
        out_ref[rows, :] = jnp.where(lane < HD, pieces[0], pieces[1]).astype(bf16)


def attend_ahead(projected):
    length, width = projected.shape[0], projected.shape[1] // 3
    pairs = width // PAIR
    block = min(512, length)

    def column(base):
        return pl.BlockSpec((length, PAIR), lambda i: (0, base + i))

    return pl.pallas_call(
        functools.partial(attend_ahead_kernel, block=block),
        grid=(pairs,),
        in_specs=[column(0), column(pairs), column(2 * pairs)],
        out_specs=[column(0), pl.BlockSpec((1, 2, length), lambda i: (i, 0, 0))],
        out_shape=[
            jax.ShapeDtypeStruct((length, width), bf16),
            jax.ShapeDtypeStruct((pairs, 2, length), f32),
        ],
        compiler_params=pltpu.CompilerParams(vmem_limit_bytes=VMEM_LIMIT),
        cost_estimate=pl.CostEstimate(
            flops=16 * length * length * width,
            bytes_accessed=8 * length * width,
            transcendentals=length * length * width // HD,
        ),
    )(projected, projected, projected)


def attend_back_kernel(
    q_ref, k_ref, v_ref, out_ref, grad_ref, log_ref, dq_ref, dk_ref, dv_ref, dk_sum, dv_sum, *, block
):
    length = q_ref.shape[0]
    lane = lax.broadcasted_iota(jnp.int32, (1, PAIR), 1)
    keys = k_ref[...]
    values = v_ref[...]
    turned = jnp.transpose(keys)
    factor = log2_e * score_scale
    for start in range(0, length, block):
        rows = pl.ds(start, block)
        queries = q_ref[rows, :]
        grads = grad_ref[rows, :]
        product = jnp.transpose(grads.astype(f32) * out_ref[rows, :].astype(f32))
        query_grads = []
        key_part = None
        value_part = None
        for h in range(2):
            mine = (lane // HD) == h
            own_q = jnp.where(mine, queries, jnp.zeros_like(queries))
            own_g = jnp.where(mine, grads, jnp.zeros_like(grads))
            inner = jnp.sum(product[h * HD : (h + 1) * HD], axis=0, keepdims=True)
            scores = mm(keys, own_q, NT)
            prob = jnp.exp2(scores * factor - log_ref[0, h, rows][None])
            grad_prob = mm(values, own_g, NT)
            grad_scores = (prob * (grad_prob - inner)).astype(bf16)
            key_term = mm(grad_scores, own_q)
            value_term = mm(prob.astype(bf16), own_g)
            key_part = key_term if key_part is None else key_part + key_term
            value_part = value_term if value_part is None else value_part + value_term
            query_grads.append(mm(turned[h * HD : (h + 1) * HD], grad_scores))
        both = jnp.transpose(jnp.concatenate(query_grads, axis=0))
        dq_ref[rows, :] = (both * score_scale).astype(bf16)
        if start == 0:
            dk_sum[...] = key_part
            dv_sum[...] = value_part
        else:
            dk_sum[...] += key_part
            dv_sum[...] += value_part
    dk_ref[...] = (dk_sum[...] * score_scale).astype(bf16)
    dv_ref[...] = dv_sum[...].astype(bf16)


def attend_back(projected, attended, grad_attended, log_total):
    length, width = projected.shape[0], projected.shape[1] // 3
    pairs = width // PAIR
    block = min(256, length)

    def column(base):
        return pl.BlockSpec((length, PAIR), lambda i: (0, base + i))

    return pl.pallas_call(
        functools.partial(attend_back_kernel, block=block),
        grid=(pairs,),
        in_specs=[
            column(0),
            column(pairs),
            column(2 * pairs),
            column(0),
            column(0),
            pl.BlockSpec((1, 2, length), lambda i: (i, 0, 0)),
        ],
        out_specs=[column(0)] * 3,
        out_shape=[jax.ShapeDtypeStruct((length, width), bf16)] * 3,
        scratch_shapes=[pltpu.VMEM((length, PAIR), f32)] * 2,
        compiler_params=pltpu.CompilerParams(vmem_limit_bytes=VMEM_LIMIT),
        cost_estimate=pl.CostEstimate(
            flops=32 * length * length * width,
            bytes_accessed=16 * length * width,
            transcendentals=length * length * width // HD,
        ),
    )(projected, projected, projected, attended, grad_attended, log_total)


def expand_kernel(x_ref, w_ref, b_ref, act_ref, slope_ref, *, block):
    length = x_ref.shape[0]
    weight = w_ref[...]
    bias = b_ref[...]
    for start in range(0, length, block):
        rows = pl.ds(start, block)
        before = mm(x_ref[rows, :], weight, NT) + bias
        phi = 0.5 * (1.0 + lax.erf(before * inv_root_two))
        act_ref[rows, :] = (before * phi).astype(bf16)
        bell = jnp.exp2(before * before * (-0.5 * log2_e)) * inv_root_tau
        slope_ref[rows, :] = (phi + before * bell).astype(bf16)


def expand_ahead(normed, weight, bias):
    length, width = normed.shape
    hidden = weight.shape[0]
    step = min(1024, hidden)
    return pl.pallas_call(
        functools.partial(expand_kernel, block=min(256, length)),
        grid=(hidden // step,),
        in_specs=[
            pl.BlockSpec((length, width), lambda i: (0, 0)),
            pl.BlockSpec((step, width), lambda i: (i, 0)),
            pl.BlockSpec((1, step), lambda i: (0, i)),
        ],
        out_specs=[pl.BlockSpec((length, step), lambda i: (0, i))] * 2,
        out_shape=[jax.ShapeDtypeStruct((length, hidden), bf16)] * 2,
        compiler_params=pltpu.CompilerParams(vmem_limit_bytes=VMEM_LIMIT),
        cost_estimate=pl.CostEstimate(
            flops=2 * length * width * hidden,
            bytes_accessed=2 * (length * width + width * hidden + 2 * length * hidden),
            transcendentals=2 * length * hidden,
        ),
    )(normed, weight, bias[None])


def normalize_parts(resid):
    centre = resid - jnp.mean(resid, axis=-1, keepdims=True)
    spread = jnp.mean(centre * centre, axis=-1, keepdims=True)
    inverse = lax.rsqrt(spread + epsilon)
    return (centre * inverse, inverse)


def normalize_back(grad_scaled, scaled, inverse):
    mean_grad = jnp.mean(grad_scaled, axis=-1, keepdims=True)
    mean_cross = jnp.mean(grad_scaled * scaled, axis=-1, keepdims=True)
    return inverse * (grad_scaled - mean_grad - scaled * mean_cross)


def layer_ahead(rows, vectors, matrices):
    triple, merge, expand, shrink = matrices
    resid = rows.astype(f32)
    scaled_one, _ = normalize_parts(resid)
    normed_one = (scaled_one * vectors["attend_gain"] + vectors["attend_shift"]).astype(bf16)
    projected = (mm(normed_one, triple, NT) + vectors["triple_bias"]).astype(bf16)
    attended, log_total = attend_ahead(projected)
    merged = mm(attended, merge) + vectors["merge_bias"]
    middle = resid + vectors["attend_scale"] * merged
    scaled_two, inverse_two = normalize_parts(middle)
    normed_two = (scaled_two * vectors["feed_gain"] + vectors["feed_shift"]).astype(bf16)
    activated, slope = expand_ahead(normed_two, expand, vectors["expand_bias"])
    shrunk = mm(activated, shrink) + vectors["shrink_bias"]
    result = middle + vectors["feed_scale"] * shrunk
    saved = (rows, normed_one, projected, attended, log_total, merged, normed_two, activated, slope, shrunk)
    return (result, saved)


def layer_back(grad_output, saved, vectors, matrices, send):
    triple, merge, expand, shrink = matrices
    rows, normed_one, projected, attended, log_total, merged, normed_two, activated, slope, shrunk = saved
    resid = rows.astype(f32)
    grads = {}
    middle = resid + vectors["attend_scale"] * merged
    scaled_one, inverse_one = normalize_parts(resid)
    scaled_two, inverse_two = normalize_parts(middle)
    grad_shrunk = (vectors["feed_scale"] * grad_output).astype(bf16)
    grads["feed_scale"] = jnp.sum(grad_output * shrunk, axis=0)
    grads["shrink_bias"] = jnp.sum(grad_shrunk.astype(f32), axis=0)
    send("shrink", mm(activated, grad_shrunk, TN).astype(bf16))
    grad_before = (mm(grad_shrunk, shrink, NT) * slope.astype(f32)).astype(bf16)
    grads["expand_bias"] = jnp.sum(grad_before.astype(f32), axis=0)
    send("expand", mm(grad_before, normed_two, TN).astype(bf16))
    product = mm(grad_before, expand)
    grads["feed_gain"] = jnp.sum(product * scaled_two, axis=0)
    grads["feed_shift"] = jnp.sum(product, axis=0)
    grad_middle = grad_output + normalize_back(product * vectors["feed_gain"], scaled_two, inverse_two)
    grad_merged = (vectors["attend_scale"] * grad_middle).astype(bf16)
    grads["attend_scale"] = jnp.sum(grad_middle * merged, axis=0)
    grads["merge_bias"] = jnp.sum(grad_merged.astype(f32), axis=0)
    send("merge", mm(attended, grad_merged, TN).astype(bf16))
    grad_attended = mm(grad_merged, merge, NT).astype(bf16)
    parts = attend_back(projected, attended, grad_attended, log_total)
    grads["triple_bias"] = jnp.concatenate(
        [jnp.sum(parts[0].astype(f32), axis=0), jnp.sum(parts[2].astype(f32), axis=0)]
    )
    width = normed_one.shape[1]
    grad_normed = jnp.zeros(resid.shape, f32)
    triple_parts = []
    for index in range(3):
        triple_parts.append(mm(parts[index], normed_one, TN).astype(bf16))
        grad_normed = grad_normed + mm(parts[index], triple[index * width : (index + 1) * width])
    send("triple", jnp.stack(triple_parts))
    grads["attend_gain"] = jnp.sum(grad_normed * scaled_one, axis=0)
    grads["attend_shift"] = jnp.sum(grad_normed, axis=0)
    grad_input = grad_middle + normalize_back(
        grad_normed * vectors["attend_gain"], scaled_one, inverse_one
    )
    return (grad_input, grads)


def gathered(piece):
    sizes = tuple(lax.axis_size(axis) for axis in EVERY)
    whole = lax.all_gather(piece, EVERY, axis=0, tiled=False)
    return whole.reshape(sizes + piece.shape)


def own_part(shard, axis):
    size = shard.shape[axis] // lax.axis_size("dp")
    return lax.dynamic_slice_in_dim(shard, lax.axis_index("dp") * size, size, axis)


def gather_weights(triple, merge, expand, shrink):
    depth = triple.shape[0]
    part = jnp.transpose(own_part(triple, 2), (1, 2, 0))
    triple_all = gathered(part)
    merge_all = gathered(own_part(merge, 0))
    expand_all = gathered(jnp.transpose(own_part(expand, 1)))
    shrink_all = gathered(own_part(shrink, 0))
    layers = []
    for layer in range(triple_all.shape[0]):
        layers.append(
            (
                jnp.transpose(triple_all[layer], (2, 0, 1, 3, 4)).reshape(-1, depth),
                merge_all[layer].reshape(-1, depth),
                expand_all[layer].reshape(-1, depth),
                shrink_all[layer].reshape(-1, depth),
            )
        )
    return layers


def scatter_grad(grad):
    sections, tensors, replicas = (lax.axis_size(axis) for axis in EVERY)
    lead, depth = grad.shape[:-2], grad.shape[-1]
    cut = grad.reshape(lead + (tensors, replicas, sections, -1, depth))
    at = len(lead)
    cut = jnp.moveaxis(cut, (at + 2, at, at + 1), (0, 1, 2))
    cut = cut.reshape((sections * tensors * replicas, -1, depth))
    return lax.psum_scatter(cut, EVERY, scatter_dimension=0, tiled=True)[0]


def body(
    boundary,
    counts,
    attend_gain,
    attend_shift,
    triple_weight,
    triple_bias,
    merge_weight,
    merge_bias,
    attend_scale,
    feed_gain,
    feed_shift,
    expand_weight,
    expand_bias,
    shrink_weight,
    shrink_bias,
    feed_scale,
):
    sections, tensors, replicas = (lax.axis_size(axis) for axis in EVERY)
    section, tensor = lax.axis_index("section"), lax.axis_index("tensor")
    members = sections * tensors
    _, micro, slots, share, depth = boundary.shape
    images = micro * slots
    assert images <= members and sections == 2

    spread = boundary[0].reshape(images, share, depth)
    spread = jnp.pad(spread, ((0, members - images), (0, 0), (0, 0)))
    received = lax.all_to_all(spread, GROUP, 0, 0, tiled=True)
    received = received.reshape(sections, tensors * share, depth)
    rows, cotangent = received[0], received[1]
    mine = section * tensors + tensor
    at = jnp.minimum(mine, images - 1)
    held = lax.dynamic_index_in_dim(counts[:, 0], at // slots, 0, keepdims=False)
    live = jnp.logical_and(mine < images, at % slots < held).astype(f32)

    matrices = gather_weights(triple_weight[0], merge_weight[0], expand_weight[0], shrink_weight[0])
    whole_bias = lax.all_gather(
        jnp.concatenate([triple_bias[0], expand_bias[0].reshape(-1, triple_bias.shape[2])]),
        "tensor",
        axis=1,
        tiled=False,
    )
    query_bias = whole_bias[0].reshape(-1)
    value_bias = whole_bias[1].reshape(-1)
    hidden_bias = jnp.moveaxis(whole_bias[2:], 1, 0).reshape(-1)
    lengths = {}
    packed = []
    for name, value in (
        ("attend_gain", attend_gain[0]),
        ("attend_shift", attend_shift[0]),
        ("triple_bias", jnp.concatenate([query_bias, jnp.zeros_like(query_bias), value_bias])),
        ("merge_bias", merge_bias[0]),
        ("attend_scale", attend_scale[0]),
        ("feed_gain", feed_gain[0]),
        ("feed_shift", feed_shift[0]),
        ("expand_bias", hidden_bias),
        ("shrink_bias", shrink_bias[0]),
        ("feed_scale", feed_scale[0]),
    ):
        lengths[name] = value.shape[0]
        packed.append(value)
    packed = lax.all_gather(jnp.concatenate(packed), "section", axis=0, tiled=False)
    vectors = []
    for layer in range(sections):
        start = 0
        named = {}
        for name, length in lengths.items():
            named[name] = packed[layer, start : start + length]
            start += length
        vectors.append(named)

    kept = []
    for layer in range(sections):
        result, saved = layer_ahead(rows, vectors[layer], matrices[layer])
        kept.append(saved)
        rows = result.astype(bf16)

    grad = cotangent.astype(f32) * live
    input_grads = [None] * sections
    vector_grads = [None] * sections
    sums = [{} for _ in range(sections)]
    for layer in reversed(range(sections)):

        def send(name, value, layer=layer):
            sums[layer][name] = scatter_grad(value)

        grad, vector_grads[layer] = layer_back(grad, kept[layer], vectors[layer], matrices[layer], send)
        input_grads[layer] = grad.astype(bf16)
        grad = input_grads[layer].astype(f32)

    returned = jnp.concatenate(input_grads).reshape(members, share, depth)
    returned = lax.all_to_all(returned, GROUP, 0, 0, tiled=True)
    boundary_grad = returned[:images].reshape(1, micro, slots, share, depth)

    names = ("triple", "merge", "expand", "shrink")
    parts = [jnp.concatenate([sums[layer][name] for name in names]) for layer in range(sections)]
    first = section == 0
    own = jnp.where(first, parts[0], parts[1])
    other = jnp.where(first, parts[1], parts[0])
    other = lax.ppermute(other, "section", [(0, 1), (1, 0)])
    halves = jnp.stack([jnp.where(first, own, other), jnp.where(first, other, own)])
    whole = lax.all_gather(halves, "dp", axis=0, tiled=False)
    cuts = {}
    start = 0
    for name in names:
        length = sums[0][name].shape[0]
        cuts[name] = whole[:, :, start : start + length].astype(f32)
        start += length
    triple_grad = cuts["triple"].reshape(replicas * sections, 3, -1, depth)
    triple_grad = jnp.transpose(triple_grad, (3, 1, 0, 2)).reshape(depth, 3, -1)
    merge_grad = cuts["merge"].reshape(-1, depth)
    expand_grad = jnp.transpose(cuts["expand"].reshape(-1, depth))
    shrink_grad = cuts["shrink"].reshape(-1, depth)

    total = lax.psum(
        jnp.stack(
            [jnp.concatenate([vector_grads[layer][name] for name in lengths if name != "triple_bias"]
                             + [vector_grads[layer]["triple_bias"]]) for layer in range(sections)]
        ),
        EVERY,
    )
    total = lax.dynamic_index_in_dim(total, section, 0, keepdims=False)
    named = {}
    start = 0
    for name in [name for name in lengths if name != "triple_bias"] + ["triple_bias"]:
        length = vector_grads[0][name].shape[0]
        named[name] = total[start : start + length]
        start += length
    expand_size = expand_bias.shape[1]
    expand_bias_grad = lax.dynamic_slice_in_dim(named["expand_bias"], tensor * expand_size, expand_size)
    bias_size = triple_bias.shape[2]
    triple_bias_grad = lax.dynamic_slice_in_dim(
        named["triple_bias"].reshape(2, -1), tensor * bias_size, bias_size, 1
    )
    return (
        boundary_grad,
        named["attend_gain"][None],
        named["attend_shift"][None],
        triple_grad[None],
        triple_bias_grad[None],
        merge_grad[None],
        named["merge_bias"][None],
        named["attend_scale"][None],
        named["feed_gain"][None],
        named["feed_shift"][None],
        expand_grad[None],
        expand_bias_grad[None],
        shrink_grad[None],
        named["shrink_bias"][None],
        named["feed_scale"][None],
    )


def solution(mesh):
    placed = (
        P("section", None, "dp", "tensor", None),
        P(None, "dp"),
        P("section", None),
        P("section", None),
        P("section", None, None, "tensor"),
        P("section", None, "tensor"),
        P("section", "tensor", None),
        P("section", None),
        P("section", None),
        P("section", None),
        P("section", None),
        P("section", None, "tensor"),
        P("section", "tensor"),
        P("section", "tensor", None),
        P("section", None),
        P("section", None),
    )
    return jax.shard_map(
        body,
        mesh=mesh,
        in_specs=placed,
        out_specs=placed[:1] + placed[2:],
        check_vma=False,
    )
```

```python
import functools
import math

import jax
import jax.numpy as jnp
from jax import lax
from jax.experimental import pallas as pl
from jax.experimental.pallas import tpu as pltpu
from jax.sharding import PartitionSpec as P

HD = 64
PAIR = 2 * HD

epsilon = 1e-06
inv_root_two = 1.0 / math.sqrt(2.0)
inv_root_tau = 1.0 / math.sqrt(2.0 * math.pi)
log2_e = math.log2(math.e)
score_scale = HD**-0.5

EVERY = ("section", "tensor", "dp")
NN = (((1,), (0,)), ((), ()))
NT = (((1,), (1,)), ((), ()))
TN = (((0,), (0,)), ((), ()))
VMEM_LIMIT = 56 << 20
COST_SHARE = 50
bf16 = jnp.bfloat16
f32 = jnp.float32


def mm(a, b, dims=NN):
    return lax.dot_general(a, b, dims, preferred_element_type=f32)


def fetch(step, blocks, slots, sems):
    depth = sems.shape[0]

    def start(k):
        for j, refs in enumerate(blocks):

            @pl.when(k == j)
            def _():
                for i, ref in enumerate(refs):
                    pltpu.make_async_copy(ref, slots[i].at[j % depth], sems.at[j % depth, i]).start()

    @pl.when(step == 0)
    def _():
        start(0)

    start(step + 1)
    slot = lax.rem(step, depth)
    for i, ref in enumerate(blocks[0]):
        pltpu.make_async_copy(ref, slots[i].at[slot], sems.at[slot, i]).wait()
    return slot


def out_copies(j, outs, refs, sems, place):
    depth = outs.shape[0]
    ref = refs[j // refs[0].shape[0]]
    for i in range(outs.shape[1]):
        for half in range(2):
            yield pltpu.make_async_copy(
                outs.at[j % depth, i, :, half],
                ref.at[j % ref.shape[0], jnp.bitwise_xor(place, half), i],
                sems.at[j % depth, i, half],
            )


def hand_out(step, count, outs, refs, sems, place):
    for j in range(count):

        @pl.when(step == j)
        def _():
            for copy in out_copies(j, outs, refs, sems, place):
                copy.start()

    @pl.when(step == count - 1)
    def _():
        for j in range(max(0, count - outs.shape[0]), count):
            for copy in out_copies(j, outs, refs, sems, place):
                copy.wait()


def slot_free(step, count, outs, refs, sems, place):
    depth = outs.shape[0]
    for j in range(depth, count):

        @pl.when(step == j)
        def _():
            for copy in out_copies(j - depth, outs, refs, sems, place):
                copy.wait()

    return lax.rem(step, depth)


def attend_pair(read, write, log_ref, length, block):
    lane = lax.broadcasted_iota(jnp.int32, (1, PAIR), 1)
    keys = read(1, pl.ds(0, length))
    values = read(2, pl.ds(0, length))
    padded = [jnp.where((lane // HD) == h, values, jnp.ones_like(values)) for h in range(2)]
    factor = log2_e * score_scale
    for start in range(0, length, block):
        rows = pl.ds(start, block)
        queries = read(0, rows)
        pieces = []
        for h in range(2):
            own = jnp.where((lane // HD) == h, queries, jnp.zeros_like(queries))
            scores = mm(own, keys, NT)
            top = jnp.max(scores, axis=1, keepdims=True) * factor
            raised = jnp.exp2(scores * factor - top).astype(bf16)
            summed = mm(raised, padded[h])
            total = summed[:, (1 - h) * HD : (1 - h) * HD + 1]
            pieces.append(summed / total)
            column = jnp.broadcast_to(top + jnp.log2(total), (block, PAIR))
            log_ref[h, rows] = jnp.transpose(column)[0]
        write(rows, jnp.where(lane < HD, pieces[0], pieces[1]).astype(bf16))


def attend_ahead_kernel(*refs, count):
    normed_ref, bias_ref = refs[:2]
    blocks = [refs[2 + j : 3 + j] for j in range(count)]
    projected_ref, attended_ref, log_ref, merged_ref, slots, sems = refs[2 + count :]
    step = pl.program_id(0)
    slot = fetch(step, blocks, [slots], sems)
    length = normed_ref.shape[0]
    width = slots.shape[2]
    for part in range(3):
        columns = pl.ds(part * width, width)
        found = mm(normed_ref[...], slots[slot, part], NT) + bias_ref[0, :, columns]
        projected_ref[0, :, columns] = found.astype(bf16)
    for pair in range(width // PAIR):
        base = pair * PAIR

        def read(part, rows, base=base):
            return projected_ref[0, rows, pl.ds(part * width + base, PAIR)]

        def write(rows, value, base=base):
            attended_ref[0, rows, pl.ds(base, PAIR)] = value

        attend_pair(read, write, log_ref.at[0, pair], length, min(512, length))
    found = mm(attended_ref[0], slots[slot, 3])

    @pl.when(step == 0)
    def _():
        merged_ref[...] = found

    @pl.when(step > 0)
    def _():
        merged_ref[...] += found


def still(shape):
    zeros = (0,) * len(shape)
    return pl.BlockSpec(shape, lambda k: zeros, pipeline_mode=pl.Buffered(buffer_count=1))


def moving(shape, offset=0):
    zeros = (0,) * (len(shape) - 1)
    return pl.BlockSpec((1,) + shape[1:], lambda k: (offset + k,) + zeros)


ANYWHERE = pl.BlockSpec(memory_space=pl.ANY)


def scalar(shape):
    return pl.BlockSpec(memory_space=pltpu.SMEM)


def slots_of(count, blocks):
    depth = min(2, count)
    return [pltpu.VMEM((depth,) + array.shape, bf16) for array in blocks[0]] + [
        pltpu.SemaphoreType.DMA((depth, len(blocks[0])))
    ]


def outs_of(count, lead, tensors, rows, depth):
    shape = (min(2, count), 2, lead, tensors, rows // (2 * tensors), depth)
    scratch = (min(2, count), lead, tensors, 2, rows // (2 * tensors), depth)
    return shape, [pltpu.VMEM(scratch, bf16), pltpu.SemaphoreType.DMA((min(2, count), lead, 2))]


def call(kernel, count, operands, outs, scratch, flops, exps):
    in_specs = [make(a.shape) if make is not None else ANYWHERE for make, a in operands]
    out_specs = [make(s) if make is not None else ANYWHERE for make, s, _ in outs]
    moved = sum(a.size * a.dtype.itemsize for _, a in operands)
    moved += sum(math.prod(s) * jnp.dtype(d).itemsize for _, s, d in outs)
    return pl.pallas_call(
        functools.partial(kernel, count=count),
        grid=(count,),
        in_specs=in_specs,
        out_specs=out_specs,
        out_shape=[jax.ShapeDtypeStruct(s, d) for _, s, d in outs],
        scratch_shapes=scratch,
        compiler_params=pltpu.CompilerParams(
            vmem_limit_bytes=VMEM_LIMIT, dimension_semantics=("arbitrary",)
        ),
        cost_estimate=pl.CostEstimate(
            flops=flops // COST_SHARE, bytes_accessed=moved // COST_SHARE, transcendentals=exps // COST_SHARE
        ),
    )(*[a for _, a in operands])


def attend_ahead(normed, bias, blocks):
    length, depth = normed.shape
    count, width = len(blocks), blocks[0][0].shape[1]
    return call(
        attend_ahead_kernel,
        count,
        [(still, normed), (moving, bias)] + [(None, array) for block in blocks for array in block],
        [
            (moving, (count, length, 3 * width), bf16),
            (moving, (count, length, width), bf16),
            (moving, (count, width // PAIR, 2, length), f32),
            (still, (length, depth), f32),
        ],
        slots_of(count, blocks),
        count * width * length * (8 * depth + 16 * length),
        count * width * length * length // HD,
    )


def attend_pair_back(read, write_query, dk_sum, dv_sum, log_ref, length, block):
    lane = lax.broadcasted_iota(jnp.int32, (1, PAIR), 1)
    keys = read(1, pl.ds(0, length))
    values = read(2, pl.ds(0, length))
    turned = jnp.transpose(keys)
    factor = log2_e * score_scale
    for start in range(0, length, block):
        rows = pl.ds(start, block)
        queries = read(0, rows)
        grads = read(4, rows)
        product = jnp.transpose(grads.astype(f32) * read(3, rows).astype(f32))
        query_grads = []
        key_part = None
        value_part = None
        for h in range(2):
            mine = (lane // HD) == h
            own_q = jnp.where(mine, queries, jnp.zeros_like(queries))
            own_g = jnp.where(mine, grads, jnp.zeros_like(grads))
            inner = jnp.sum(product[h * HD : (h + 1) * HD], axis=0, keepdims=True)
            scores = mm(keys, own_q, NT)
            prob = jnp.exp2(scores * factor - log_ref[h, rows][None])
            grad_prob = mm(values, own_g, NT)
            grad_scores = (prob * (grad_prob - inner)).astype(bf16)
            key_term = mm(grad_scores, own_q)
            value_term = mm(prob.astype(bf16), own_g)
            key_part = key_term if key_part is None else key_part + key_term
            value_part = value_term if value_part is None else value_part + value_term
            query_grads.append(mm(turned[h * HD : (h + 1) * HD], grad_scores))
        both = jnp.transpose(jnp.concatenate(query_grads, axis=0))
        write_query(rows, (both * score_scale).astype(bf16))
        if start == 0:
            dk_sum[...] = key_part
            dv_sum[...] = value_part
        else:
            dk_sum[...] += key_part
            dv_sum[...] += value_part


def attend_back_kernel(*refs, count):
    place_ref, grad_ref, normed_ref, projected_ref, attended_ref, log_ref = refs[:6]
    blocks = [refs[6 + j : 7 + j] for j in range(count)]
    out_refs, refs = refs[6 + count : -10], refs[-10:]
    sums_ref, total_ref, slots, sems, outs, out_sems, inward, parts, dk_sum, dv_sum = refs
    step = pl.program_id(0)
    place = place_ref[0]
    slot = fetch(step, blocks, [slots], sems)
    out = slot_free(step, count, outs, out_refs, out_sems, place)
    length = normed_ref.shape[0]
    width = slots.shape[2]
    inward[...] = mm(grad_ref[...], slots[slot, 3], NT).astype(bf16)
    for pair in range(width // PAIR):
        base = pair * PAIR

        def read(part, rows, base=base):
            if part == 3:
                return attended_ref[0, rows, pl.ds(base, PAIR)]
            if part == 4:
                return inward[rows, pl.ds(base, PAIR)]
            return projected_ref[0, rows, pl.ds(part * width + base, PAIR)]

        def write_query(rows, value, base=base):
            parts[rows, pl.ds(base, PAIR)] = value

        attend_pair_back(
            read, write_query, dk_sum, dv_sum, log_ref.at[0, pair], length, min(256, length)
        )
        parts[:, pl.ds(width + base, PAIR)] = (dk_sum[...] * score_scale).astype(bf16)
        parts[:, pl.ds(2 * width + base, PAIR)] = dv_sum[...].astype(bf16)
    found = None
    for part in range(3):
        columns = pl.ds(part * width, width)
        outs[out, part] = mm(parts[:, columns], normed_ref[...], TN).astype(bf16).reshape(outs.shape[2:])
        sums_ref[0, :, columns] = jnp.sum(parts[:, columns].astype(f32), axis=0, keepdims=True)
        term = mm(parts[:, columns], slots[slot, part])
        found = term if found is None else found + term
    outs[out, 3] = mm(attended_ref[0], grad_ref[...], TN).astype(bf16).reshape(outs.shape[2:])
    hand_out(step, count, outs, out_refs, out_sems, place)

    @pl.when(step == 0)
    def _():
        total_ref[...] = found

    @pl.when(step > 0)
    def _():
        total_ref[...] += found


def attend_back(place, tensors, grad_merged, normed, projected, attended, logs, blocks, offset):
    length, depth = normed.shape
    count, width = len(blocks), blocks[0][0].shape[1]
    at = functools.partial(moving, offset=offset)
    shape, outs = outs_of(count, 4, tensors, width, depth)
    results = call(
        attend_back_kernel,
        count,
        [(scalar, place), (still, grad_merged), (still, normed)]
        + [(at, projected), (at, attended), (at, logs)]
        + [(None, array) for block in blocks for array in block],
        [(None, shape, bf16)] * max(1, count // 2)
        + [(moving, (count, 1, 3 * width), f32), (still, (length, depth), f32)],
        slots_of(count, blocks)
        + outs
        + [
            pltpu.VMEM((length, width), bf16),
            pltpu.VMEM((length, 3 * width), bf16),
            pltpu.VMEM((length, PAIR), f32),
            pltpu.VMEM((length, PAIR), f32),
        ],
        count * width * length * (16 * depth + 32 * length),
        count * width * length * length // HD,
    )
    return results[:-2], results[-2], results[-1]


def feed_ahead_kernel(*refs, count):
    normed_ref, bias_ref = refs[:2]
    blocks = [refs[2 + 2 * j : 4 + 2 * j] for j in range(count)]
    act_ref, slope_ref, total_ref, expand, shrink, sems = refs[2 + 2 * count :]
    step = pl.program_id(0)
    slot = fetch(step, blocks, [expand, shrink], sems)
    length = normed_ref.shape[0]
    block = min(256, length)
    bias = bias_ref[0]
    for start in range(0, length, block):
        rows = pl.ds(start, block)
        before = mm(normed_ref[rows, :], expand[slot], NT) + bias
        phi = 0.5 * (1.0 + lax.erf(before * inv_root_two))
        act_ref[0, rows, :] = (before * phi).astype(bf16)
        bell = jnp.exp2(before * before * (-0.5 * log2_e)) * inv_root_tau
        slope_ref[0, rows, :] = (phi + before * bell).astype(bf16)
    found = mm(act_ref[0], shrink[slot])

    @pl.when(step == 0)
    def _():
        total_ref[...] = found

    @pl.when(step > 0)
    def _():
        total_ref[...] += found


def feed_ahead(normed, bias, blocks):
    length, depth = normed.shape
    count, hidden = len(blocks), blocks[0][0].shape[0]
    return call(
        feed_ahead_kernel,
        count,
        [(still, normed), (moving, bias)] + [(None, array) for block in blocks for array in block],
        [
            (moving, (count, length, hidden), bf16),
            (moving, (count, length, hidden), bf16),
            (still, (length, depth), f32),
        ],
        slots_of(count, blocks),
        4 * count * hidden * length * depth,
        2 * count * hidden * length,
    )


def feed_back_kernel(*refs, count):
    place_ref, grad_ref, normed_ref, act_ref, slope_ref = refs[:5]
    blocks = [refs[5 + 2 * j : 7 + 2 * j] for j in range(count)]
    out_refs, refs = refs[5 + 2 * count : -8], refs[-8:]
    sums_ref, total_ref, expand, shrink, sems, outs, out_sems, inward = refs
    step = pl.program_id(0)
    place = place_ref[0]
    slot = fetch(step, blocks, [expand, shrink], sems)
    out = slot_free(step, count, outs, out_refs, out_sems, place)
    length = normed_ref.shape[0]
    block = min(256, length)
    outs[out, 1] = mm(act_ref[0], grad_ref[...], TN).astype(bf16).reshape(outs.shape[2:])
    summed = None
    for start in range(0, length, block):
        rows = pl.ds(start, block)
        before = mm(grad_ref[rows, :], shrink[slot], NT) * slope_ref[0, rows, :].astype(f32)
        before = before.astype(bf16)
        inward[rows, :] = before
        part = jnp.sum(before.astype(f32), axis=0, keepdims=True)
        summed = part if summed is None else summed + part
    sums_ref[0] = summed
    outs[out, 0] = mm(inward[...], normed_ref[...], TN).astype(bf16).reshape(outs.shape[2:])
    hand_out(step, count, outs, out_refs, out_sems, place)
    found = mm(inward[...], expand[slot])

    @pl.when(step == 0)
    def _():
        total_ref[...] = found

    @pl.when(step > 0)
    def _():
        total_ref[...] += found


def feed_back(place, tensors, grad_shrunk, normed, activated, slope, blocks, offset):
    length, depth = normed.shape
    count, hidden = len(blocks), blocks[0][0].shape[0]
    at = functools.partial(moving, offset=offset)
    shape, outs = outs_of(count, 2, tensors, hidden, depth)
    results = call(
        feed_back_kernel,
        count,
        [(scalar, place), (still, grad_shrunk), (still, normed), (at, activated), (at, slope)]
        + [(None, array) for block in blocks for array in block],
        [(None, shape, bf16)] * max(1, count // 2)
        + [(moving, (count, 1, hidden), f32), (still, (length, depth), f32)],
        slots_of(count, blocks) + outs + [pltpu.VMEM((length, hidden), bf16)],
        8 * count * hidden * length * depth,
        0,
    )
    return results[:-2], results[-2], results[-1]


def swapped(value, axis, bits):
    count = lax.axis_size(axis)
    flat = value.reshape(-1, value.shape[-1])
    flat = lax.ppermute(flat, axis, [(i, i ^ bits) for i in range(count)])
    return flat.reshape(value.shape)


def is_first():
    return lax.axis_index("section") == 0


def tie(*values):
    return lax.optimization_barrier(values)


def spread(value, axis):
    whole = value[None]
    for bit in (1 << i for i in range(lax.axis_size(axis).bit_length() - 1)):
        other = swapped(whole, axis, bit)
        low = (lax.axis_index(axis) & bit) == 0
        whole = jnp.concatenate([jnp.where(low, whole, other), jnp.where(low, other, whole)])
    return whole


def own_part(shard, axis, split):
    if not split:
        return shard
    size = shard.shape[axis] // lax.axis_size("dp")
    return lax.dynamic_slice_in_dim(shard, lax.axis_index("dp") * size, size, axis)


def exchanged(values):
    return lax.all_to_all(values, "tensor", 0, 0, tiled=True)


def plus(a, b):
    return (a.astype(f32) + b.astype(f32)).astype(bf16)


class Scatter:
    def __init__(self, layer):
        self.layer = layer

    def start(self, odd, even):
        self.even = even
        self.got = swapped(odd, "dp", 1)
        self.stage = self.one

    def one(self, got):
        half = self.even.shape[2] // 2
        keep = plus(self.even[:, 0, :half], got[:, 0, :half])
        send = plus(self.even[:, 1, :half], got[:, 1, :half])
        stay = plus(self.even[0, :, half:], got[0, :, half:])
        leave = plus(self.even[1, :, half:], got[1, :, half:])
        return (keep, stay, send, leave)

    def after_one(self, outs):
        self.keep, self.stay, send, leave = outs
        self.got = (swapped(send, "section", 1), swapped(leave, "dp", 2))
        self.stage = self.two

    def two(self, got):
        mine, leave = plus(self.keep[0], got[0][0]), plus(self.keep[1], got[0][1])
        return (mine, plus(self.stay[0], got[1][0]), leave, plus(self.stay[1], got[1][1]))

    def after_two(self, outs):
        self.mine, self.stay, leave, send = outs
        self.got = (swapped(leave, "dp", 2), swapped(send, "section", 1))
        self.stage = self.three

    def three(self, got):
        whole = jnp.concatenate([plus(self.mine, got[0]), plus(self.stay, got[1])])
        lead, tensors, rows, depth = whole.shape
        return jnp.transpose(whole, (1, 0, 2, 3)).reshape(tensors, lead * rows, depth)

    def after_three(self, whole):
        lead = 2 * self.mine.shape[0]
        piece = lax.psum_scatter(whole, "tensor", scatter_dimension=0, tiled=True)
        self.got = piece.reshape(lead, -1, whole.shape[-1])
        self.stage = self.four

    def four(self, got):
        return got

    def after_four(self, piece):
        self.piece = piece
        self.got = lax.ppermute(piece, "section", [(1 - self.layer, self.layer)])
        self.stage = self.end

    def end(self, got):
        first = is_first()
        low = jnp.where(first, self.piece, got)
        return jnp.concatenate([low, jnp.where(first, got, self.piece)], axis=1)

    def after_end(self, shard):
        self.shard = shard

    def whole_sum(self, block):
        whole = lax.psum(block, "dp")
        piece = lax.psum_scatter(whole, "tensor", scatter_dimension=2, tiled=True)[:, :, 0]
        first = is_first()
        piece = jnp.stack([jnp.where(first, piece[0], piece[1]), jnp.where(first, piece[1], piece[0])])
        piece = plus(piece, lax.ppermute(piece, "section", [(1 - self.layer, self.layer)]))
        self.shard = jnp.concatenate([piece[0], piece[1]], axis=1)


class Join:
    def __init__(self, piece):
        self.piece = piece
        self.got = swapped(piece, "dp", 2)
        self.stage = self.far

    def far(self, got):
        low = (lax.axis_index("dp") & 2) == 0
        return jnp.stack([jnp.where(low, self.piece, got), jnp.where(low, got, self.piece)])

    def after_far(self, pair):
        self.pair = pair
        self.got = swapped(pair, "dp", 1)
        self.stage = self.near

    def near(self, got):
        low = (lax.axis_index("dp") & 1) == 0
        even, odd = jnp.where(low, self.pair, got), jnp.where(low, got, self.pair)
        return [even[0], odd[0], even[1], odd[1]]

    def after_near(self, parts):
        self.parts = parts


class Return:
    def __init__(self, layer, grad, tensors):
        self.layer = layer
        self.got = exchanged(grad.reshape(tensors, -1, grad.shape[1]))
        self.stage = self.over

    def over(self, got):
        return got

    def after_over(self, cut):
        self.cut = cut
        self.other = lax.ppermute(cut, "section", [(1 - self.layer, self.layer)])


class Total:
    def __init__(self, value):
        self.bits = [
            (axis, 1 << i)
            for axis in ("dp", "tensor", "section")
            for i in range(lax.axis_size(axis).bit_length() - 1)
        ]
        self.send(value)

    def send(self, value):
        self.value = value
        if self.bits:
            self.got = swapped(value, *self.bits.pop(0))
        self.stage = self.add

    def add(self, got):
        return self.value + got

    def after_add(self, value):
        self.send(value)


def advance(chain, *jobs):
    got, chain = tie([job.got for job in jobs], chain)
    stages = [job.stage for job in jobs]
    outs = [stage(value) for stage, value in zip(stages, got)]
    outs, chain = tie(outs, chain)
    for job, stage, out in zip(jobs, stages, outs):
        getattr(job, "after_" + stage.__name__)(out)
    return chain


def normalize_parts(resid):
    centre = resid - jnp.mean(resid, axis=-1, keepdims=True)
    spread = jnp.mean(centre * centre, axis=-1, keepdims=True)
    inverse = lax.rsqrt(spread + epsilon)
    return (centre * inverse, inverse)


def normalize_back(grad_scaled, scaled, inverse):
    mean_grad = jnp.mean(grad_scaled, axis=-1, keepdims=True)
    mean_cross = jnp.mean(grad_scaled * scaled, axis=-1, keepdims=True)
    return inverse * (grad_scaled - mean_grad - scaled * mean_cross)


def block_order(blocks):
    return sorted(blocks, key=lambda k: (k + 1) % 2)


def in_groups(blocks, count):
    order = block_order(blocks)
    size = len(order) // min(count, len(order))
    return [(start, order[start : start + size]) for start in range(0, len(order), size)]


def attend_half(rows, vectors, blocks):
    resid = rows.astype(f32)
    scaled_one, _ = normalize_parts(resid)
    normed_one = (scaled_one * vectors["attend_gain"] + vectors["attend_shift"]).astype(bf16)
    order = block_order(blocks)
    bias = jnp.stack([vectors["triple_bias"][k] for k in order])[:, None]
    projected, attended, logs, merged = attend_ahead(normed_one, bias, [blocks[k] for k in order])
    return (normed_one, projected, attended, logs, merged)


def feed_half(rows, merged, vectors, blocks):
    merged = merged + vectors["merge_bias"]
    middle = rows.astype(f32) + vectors["attend_scale"] * merged
    scaled_two, _ = normalize_parts(middle)
    normed_two = (scaled_two * vectors["feed_gain"] + vectors["feed_shift"]).astype(bf16)
    order = block_order(blocks)
    bias = jnp.stack([vectors["expand_bias"][k] for k in order])[:, None]
    activated, slope, shrunk = feed_ahead(normed_two, bias, [blocks[k] for k in order])
    shrunk = shrunk + vectors["shrink_bias"]
    result = (middle + vectors["feed_scale"] * shrunk).astype(bf16)
    return (result, merged, normed_two, activated, slope, shrunk)


def layer_back(place, tensors, grad_output, saved, vectors, attend_blocks, feed_blocks, sums, hooks):
    rows, normed_one, projected, attended, logs, merged, normed_two, activated, slope, shrunk = saved
    grads = {}
    grad_wide = grad_output.astype(f32)
    grad_shrunk = (vectors["feed_scale"] * grad_wide).astype(bf16)
    grads["feed_scale"] = jnp.sum(grad_wide * shrunk, axis=0)
    grads["shrink_bias"] = jnp.sum(grad_shrunk.astype(f32), axis=0)

    order = block_order(feed_blocks)
    parts, columns, product = feed_back(
        place, tensors, grad_shrunk, normed_two, activated, slope, [feed_blocks[k] for k in order], 0
    )
    grads["expand_bias"] = {k: columns[i] for i, k in enumerate(order)}
    product = hooks["kernel"](product)
    sums["feed"].start(*parts)

    resid = rows.astype(f32)
    middle = resid + vectors["attend_scale"] * merged
    scaled_one, inverse_one = normalize_parts(resid)
    scaled_two, inverse_two = normalize_parts(middle)
    grads["feed_gain"] = jnp.sum(product * scaled_two, axis=0)
    grads["feed_shift"] = jnp.sum(product, axis=0)
    grad_middle = grad_wide + normalize_back(product * vectors["feed_gain"], scaled_two, inverse_two)
    grad_merged = (vectors["attend_scale"] * grad_middle).astype(bf16)
    grads["attend_scale"] = jnp.sum(grad_middle * merged, axis=0)
    grads["merge_bias"] = jnp.sum(grad_merged.astype(f32), axis=0)
    grad_merged = hooks["feed"](grad_merged)

    total = None
    grads["triple_bias"] = {}
    parts = []
    groups = in_groups(attend_blocks, hooks["groups"])
    for i, (offset, ks) in enumerate(groups):
        found_parts, columns, found = attend_back(
            place, tensors, grad_merged, normed_one, projected, attended, logs,
            [attend_blocks[k] for k in ks], offset,
        )
        for j, k in enumerate(ks):
            cut = columns[j].reshape(3, -1)
            grads["triple_bias"][k] = jnp.stack([cut[0], cut[2]])
        parts.extend(found_parts)
        if i == 0 and len(groups) == 2:
            parts, grad_merged, found = tie(parts, grad_merged, found)
            sums["attend"].start(parts[0], None)
            grad_merged = hooks["midway"](grad_merged)
        total = found if total is None else total + found
    if len(parts) == 1:
        sums["attend"].whole_sum(parts[0][0])
    elif len(groups) == 2:
        sums["attend"].even = parts[1]
    else:
        sums["attend"].start(*parts)
    total = hooks["attend"](total)
    grads["attend_gain"] = jnp.sum(total * scaled_one, axis=0)
    grads["attend_shift"] = jnp.sum(total, axis=0)
    grad_input = grad_middle + normalize_back(total * vectors["attend_gain"], scaled_one, inverse_one)
    return (hooks["end"](grad_input.astype(bf16)), grads)


def body(
    boundary,
    counts,
    attend_gain,
    attend_shift,
    triple_weight,
    triple_bias,
    merge_weight,
    merge_bias,
    attend_scale,
    feed_gain,
    feed_shift,
    expand_weight,
    expand_bias,
    shrink_weight,
    shrink_bias,
    feed_scale,
):
    sections, tensors, replicas = (lax.axis_size(axis) for axis in EVERY)
    section, tensor, replica = (lax.axis_index(axis) for axis in EVERY)
    first = section == 0
    members = sections * tensors
    _, micro, slots, share, depth = boundary.shape
    images = micro * slots
    assert images <= members and sections == 2 and replicas == 4
    heads_split = (triple_bias.shape[2] // HD) % replicas == 0

    attend_piece = jnp.concatenate(
        [
            jnp.transpose(own_part(triple_weight[0], 2, heads_split), (1, 2, 0)),
            own_part(merge_weight[0], 0, heads_split)[None],
        ]
    )
    expand_piece = jnp.transpose(own_part(expand_weight[0], 1, True))
    shrink_piece = own_part(shrink_weight[0], 0, True)

    spread_rows = boundary[0].reshape(images, share, depth)
    spread_rows = jnp.pad(spread_rows, ((0, members - images), (0, 0), (0, 0)))
    near, far = spread_rows[:tensors], spread_rows[tensors:]
    leaving = jnp.where(first, far, near)

    home = lax.all_gather(attend_piece, "tensor", axis=1, tiled=True)
    other_expand = swapped(expand_piece, "section", 1)
    leaving, other_expand = tie(leaving, other_expand)
    passed = swapped(leaving, "section", 1)

    def whole(layer, own, other):
        return lax.all_gather(jnp.where(section == layer, own, other), "tensor", axis=0, tiled=True)

    expand_own = [whole(0, expand_piece, other_expand)]
    home, passed, shrink_piece = tie(home, passed, shrink_piece)
    rows = exchanged(jnp.where(first, near, passed))
    foreign = swapped(home, "section", 1)
    beyond = swapped(home, "dp", 2) if heads_split else home
    other_shrink = swapped(shrink_piece, "section", 1)
    rows, beyond, other_shrink, expand_own[0] = tie(rows, beyond, other_shrink, expand_own[0])
    foreign_beyond = swapped(beyond, "section", 1) if heads_split else foreign
    shrink_own = [whole(0, shrink_piece, other_shrink)]
    expand_own.append(whole(1, expand_piece, other_expand))
    shrink_own.append(whole(1, shrink_piece, other_shrink))
    rows = rows.reshape(tensors * share, depth)
    cotangent = jnp.where(first, passed, far)
    mine = section * tensors + tensor
    at = jnp.minimum(mine, images - 1)
    held = lax.dynamic_index_in_dim(counts[:, 0], at // slots, 0, keepdims=False)
    live = jnp.logical_and(mine < images, at % slots < held)

    def both(home, foreign):
        return jnp.where(first, home, foreign), jnp.where(first, foreign, home)

    attend_blocks = [{}, {}]
    for k, pair in ((0, both(home, foreign)), (2, both(beyond, foreign_beyond)))[: 2 if heads_split else 1]:
        for layer in range(sections):
            attend_blocks[layer][k] = (pair[layer],)
            if heads_split:
                attend_blocks[layer][k + 1] = (swapped(pair[layer], "dp", 1),)

    def around(value):
        return {0: value, 1: swapped(value, "dp", 1), 2: swapped(value, "dp", 2)}

    def full(blocks):
        return {**blocks, 3: swapped(blocks[2], "dp", 1)}

    def paired(expand, shrink):
        return {k: (expand[k], shrink[k]) for k in expand}

    biases = spread(jnp.concatenate([triple_bias[0].reshape(-1), expand_bias[0]]), "tensor")
    names = (
        "attend_gain",
        "attend_shift",
        "merge_bias",
        "attend_scale",
        "feed_gain",
        "feed_shift",
        "shrink_bias",
        "feed_scale",
    )
    plain = (
        attend_gain,
        attend_shift,
        merge_bias,
        attend_scale,
        feed_gain,
        feed_shift,
        shrink_bias,
        feed_scale,
    )
    small = spread(jnp.concatenate([value[0] for value in plain] + [biases.reshape(-1)]), "section")

    def block_part(value, axis, which):
        size = value.shape[axis] // replicas
        return lax.dynamic_slice_in_dim(value, jnp.bitwise_xor(replica, which) * size, size, axis)

    vectors = []
    for layer in range(sections):
        named = {name: small[layer, i * depth : (i + 1) * depth] for i, name in enumerate(names)}
        by_tensor = small[layer, len(names) * depth :].reshape(tensors, -1)
        width = triple_bias.shape[2]
        query, value, hidden = (
            by_tensor[:, :width],
            by_tensor[:, width : 2 * width],
            by_tensor[:, 2 * width :],
        )
        named["triple_bias"] = {}
        for k in attend_blocks[layer]:
            q_part, v_part = query, value
            if heads_split:
                q_part, v_part = block_part(query, 1, k), block_part(value, 1, k)
            q_part, v_part = q_part.reshape(-1), v_part.reshape(-1)
            named["triple_bias"][k] = jnp.concatenate([q_part, jnp.zeros_like(q_part), v_part])
        named["expand_bias"] = {k: block_part(hidden, 1, k).reshape(-1) for k in range(replicas)}
        vectors.append(named)

    expand_next = around(expand_own[0])
    shrink_own[0], expand_next, rows = tie(shrink_own[0], expand_next, rows)
    shrink_next = around(shrink_own[0])
    normed, projected, attended, logs, merged = attend_half(rows, vectors[0], attend_blocks[0])
    shrink_next, attend_blocks[1], expand_own[1], merged = tie(
        shrink_next, attend_blocks[1], expand_own[1], merged
    )
    blocks = paired(full(expand_next), full(shrink_next))
    expand_next = around(expand_own[1])
    result, merged, normed_two, activated, slope, shrunk = feed_half(rows, merged, vectors[0], blocks)
    feed_blocks = [blocks]
    kept = [(rows, normed, projected, attended, logs, merged, normed_two, activated, slope, shrunk)]
    expand_next, shrink_own[1], cotangent, rows = tie(expand_next, shrink_own[1], cotangent, result)
    shrink_next = around(shrink_own[1])
    cotangent = exchanged(cotangent)
    normed, projected, attended, logs, merged = attend_half(rows, vectors[1], attend_blocks[1])
    shrink_next, cotangent, merged = tie(shrink_next, cotangent, merged)
    blocks = paired(full(expand_next), full(shrink_next))
    _, merged, normed_two, activated, slope, shrunk = feed_half(rows, merged, vectors[1], blocks)
    feed_blocks.append(blocks)
    kept.append((rows, normed, projected, attended, logs, merged, normed_two, activated, slope, shrunk))
    cotangent = cotangent.reshape(tensors * share, depth)
    cotangent = jnp.where(live, cotangent, jnp.zeros_like(cotangent))

    def whole_of(blocks):
        rows_of = blocks[0].shape[0]
        cuts = jnp.stack([blocks[k].reshape(rows_of, tensors, -1) for k in sorted(blocks)], axis=2)
        if len(blocks) == 1:
            return cuts.reshape(-1)
        order = jnp.bitwise_xor(replica, jnp.arange(replicas))
        return jnp.take(cuts, order, axis=2).reshape(-1)

    place = section.astype(jnp.int32).reshape(1)
    sums = [{"attend": Scatter(layer), "feed": Scatter(layer)} for layer in range(sections)]
    feed, attend = [found["feed"] for found in sums], [found["attend"] for found in sums]
    attend_jobs = (lambda layer: [attend[layer]]) if heads_split else (lambda layer: [])
    extra = {}

    def packed(layer):
        found = vector_grads[layer]
        return jnp.concatenate(
            [found[name] for name in names]
            + [whole_of(found["triple_bias"]), whole_of(found["expand_bias"])]
        )

    def after_second(grad):
        grad = advance(grad, *attend_jobs(1))
        extra[1] = Return(1, grad, tensors)
        return grad

    hooks = {
        "groups": 1,
        "kernel": lambda chain: chain,
        "feed": lambda chain: advance(chain, feed[1]),
        "attend": lambda chain: advance(chain, feed[1]),
        "end": after_second,
    }
    vector_grads = [None] * sections
    grad, vector_grads[1] = layer_back(
        place, tensors, cotangent, kept[1], vectors[1], attend_blocks[1], feed_blocks[1], sums[1], hooks
    )
    gathered_total = lax.all_gather(packed(1), EVERY, axis=0, tiled=False)

    def midway(chain):
        extra["total"], chain = tie(gathered_total, chain)
        return advance(chain, feed[0], feed[1], *attend_jobs(1))

    def after_first(grad):
        extra[0] = Return(0, grad, tensors)
        return grad

    hooks = {
        "groups": 2,
        "kernel": lambda chain: advance(chain, feed[1], extra[1], *attend_jobs(1)),
        "feed": lambda chain: advance(chain, feed[0]),
        "midway": midway,
        "attend": lambda chain: advance(chain, feed[0], feed[1], *attend_jobs(0)),
        "end": after_first,
    }
    if not heads_split:
        hooks["attend"] = lambda chain: advance(midway(chain), feed[0], feed[1])
    chain, vector_grads[0] = layer_back(
        place, tensors, grad, kept[0], vectors[0], attend_blocks[0], feed_blocks[0], sums[0], hooks
    )
    last = Total(packed(0))
    chain = advance(chain, last, *attend_jobs(0))
    chain = advance(chain, last, feed[0], *attend_jobs(0))
    chain = advance(chain, extra[0], feed[0], *attend_jobs(1))
    feed_join = Join(jnp.where(first, feed[0].shard, feed[1].shard))
    if heads_split:
        chain = advance(chain, last, attend[0])
        chain = advance(chain, attend[0], attend[1])
        attend_join = Join(jnp.where(first, attend[0].shard, attend[1].shard))
        chain = advance(chain, feed_join)
        chain = advance(chain, last, feed_join, attend_join)
        chain = advance(chain, last, attend_join)
        attend_parts = attend_join.parts
    else:
        chain = advance(advance(chain, feed_join, last), feed_join)
        attend_parts = [jnp.where(first, attend[0].shard, attend[1].shard)]
        while last.bits:
            chain = advance(chain, last)
        chain = advance(chain, last)
    near = jnp.where(first, extra[0].cut, extra[1].other)
    far = jnp.where(first, extra[0].other, extra[1].cut)
    boundary_grad = jnp.concatenate([near, far])[:images].reshape(1, micro, slots, share, depth)
    total = jnp.where(first, last.value, jnp.sum(extra["total"], axis=0))

    triple_grad = jnp.concatenate([part[:3] for part in attend_parts], axis=1)
    triple_grad = jnp.transpose(triple_grad.astype(f32), (2, 0, 1))
    merge_grad = jnp.concatenate([part[3] for part in attend_parts]).astype(f32)
    expand_grad = jnp.concatenate([part[0] for part in feed_join.parts])
    expand_grad = jnp.transpose(expand_grad.astype(f32))
    shrink_grad = jnp.concatenate([part[1] for part in feed_join.parts]).astype(f32)

    named = {name: total[i * depth : (i + 1) * depth] for i, name in enumerate(names)}
    rest = total[len(names) * depth :]
    bias_width, hidden_width = triple_bias.shape[2], expand_bias.shape[1]
    pair = rest[: 2 * tensors * bias_width].reshape(2, -1)
    triple_bias_grad = lax.dynamic_slice_in_dim(pair, tensor * bias_width, bias_width, 1)
    expand_bias_grad = lax.dynamic_slice_in_dim(
        rest[2 * tensors * bias_width :], tensor * hidden_width, hidden_width
    )
    return (
        boundary_grad,
        named["attend_gain"][None],
        named["attend_shift"][None],
        triple_grad[None],
        triple_bias_grad[None],
        merge_grad[None],
        named["merge_bias"][None],
        named["attend_scale"][None],
        named["feed_gain"][None],
        named["feed_shift"][None],
        expand_grad[None],
        expand_bias_grad[None],
        shrink_grad[None],
        named["shrink_bias"][None],
        named["feed_scale"][None],
    )


def solution(mesh):
    placed = (
        P("section", None, "dp", "tensor", None),
        P(None, "dp"),
        P("section", None),
        P("section", None),
        P("section", None, None, "tensor"),
        P("section", None, "tensor"),
        P("section", "tensor", None),
        P("section", None),
        P("section", None),
        P("section", None),
        P("section", None),
        P("section", None, "tensor"),
        P("section", "tensor"),
        P("section", "tensor", None),
        P("section", None),
        P("section", None),
    )
    return jax.shard_map(
        body,
        mesh=mesh,
        in_specs=placed,
        out_specs=placed[:1] + placed[2:],
        check_vma=False,
    )
```

```python
import functools
import math

import jax
import jax.numpy as jnp
from jax import lax
from jax.experimental import pallas as pl
from jax.experimental.pallas import tpu as pltpu
from jax.sharding import PartitionSpec as P

HD = 64
PAIR = 2 * HD

epsilon = 1e-06
inv_root_two = 1.0 / math.sqrt(2.0)
inv_root_tau = 1.0 / math.sqrt(2.0 * math.pi)
log2_e = math.log2(math.e)
score_scale = HD**-0.5

SECTION, TENSOR, DP = "section", "tensor", "dp"
EVERY = (SECTION, TENSOR, DP)
ATTEND = "attend"
FEED = "feed"
TOTAL = "total"
EXPAND_BIAS = "expand_bias"
TRIPLE_BIAS = "triple_bias"
KERNEL = "kernel"
MIDWAY = "midway"
GROUPS = "groups"
END = "end"
ATTEND_GAIN = "attend_gain"
FEED_GAIN = "feed_gain"
ATTEND_SCALE = "attend_scale"
FEED_SCALE = "feed_scale"
MERGE_BIAS = "merge_bias"
SHRINK_BIAS = "shrink_bias"
ATTEND_SHIFT = "attend_shift"
FEED_SHIFT = "feed_shift"
NN = (((1,), (0,)), ((), ()))
NT = (((1,), (1,)), ((), ()))
TN = (((0,), (0,)), ((), ()))
VMEM_LIMIT = 56 << 20
COST_SHARE = 50
bf16 = jnp.bfloat16
f32 = jnp.float32


def mm(a, b, dims=NN):
    return lax.dot_general(a, b, dims, preferred_element_type=f32)


def fetch(step, blocks, slots, sems):
    depth = sems.shape[0]

    def start(k):
        for j, refs in enumerate(blocks):

            @pl.when(k == j)
            def _():
                for i, ref in enumerate(refs):
                    pltpu.make_async_copy(ref, slots[i].at[j % depth], sems.at[j % depth, i]).start()

    @pl.when(step == 0)
    def _():
        start(0)

    start(step + 1)
    slot = lax.rem(step, depth)
    for i, ref in enumerate(blocks[0]):
        pltpu.make_async_copy(ref, slots[i].at[slot], sems.at[slot, i]).wait()
    return slot


def out_copies(j, outs, refs, sems, place):
    depth = outs.shape[0]
    ref = refs[j // refs[0].shape[0]]
    for i in range(outs.shape[1]):
        for half in range(2):
            yield pltpu.make_async_copy(
                outs.at[j % depth, i, :, half],
                ref.at[j % ref.shape[0], jnp.bitwise_xor(place, half), i],
                sems.at[j % depth, i, half],
            )


def hand_out(step, count, outs, refs, sems, place):
    for j in range(count):

        @pl.when(step == j)
        def _():
            for copy in out_copies(j, outs, refs, sems, place):
                copy.start()

    @pl.when(step == count - 1)
    def _():
        for j in range(max(0, count - outs.shape[0]), count):
            for copy in out_copies(j, outs, refs, sems, place):
                copy.wait()


def slot_free(step, count, outs, refs, sems, place):
    depth = outs.shape[0]
    for j in range(depth, count):

        @pl.when(step == j)
        def _():
            for copy in out_copies(j - depth, outs, refs, sems, place):
                copy.wait()

    return lax.rem(step, depth)


def attend_pair(read, write, log_ref, length, block):
    lane = lax.broadcasted_iota(jnp.int32, (1, PAIR), 1)
    keys = read(1, pl.ds(0, length))
    values = read(2, pl.ds(0, length))
    padded = [jnp.where((lane // HD) == h, values, jnp.ones_like(values)) for h in range(2)]
    factor = log2_e * score_scale
    for start in range(0, length, block):
        rows = pl.ds(start, block)
        queries = read(0, rows)
        pieces = []
        for h in range(2):
            own = jnp.where((lane // HD) == h, queries, jnp.zeros_like(queries))
            scores = mm(own, keys, NT)
            top = jnp.max(scores, axis=1, keepdims=True) * factor
            raised = jnp.exp2(scores * factor - top).astype(bf16)
            summed = mm(raised, padded[h])
            total = summed[:, (1 - h) * HD : (1 - h) * HD + 1]
            pieces.append(summed / total)
            column = jnp.broadcast_to(top + jnp.log2(total), (block, PAIR))
            log_ref[h, rows] = jnp.transpose(column)[0]
        write(rows, jnp.where(lane < HD, pieces[0], pieces[1]).astype(bf16))


def attend_ahead_kernel(*refs, count):
    normed_ref, bias_ref = refs[:2]
    blocks = [refs[2 + j : 3 + j] for j in range(count)]
    projected_ref, attended_ref, log_ref, merged_ref, slots, sems = refs[2 + count :]
    step = pl.program_id(0)
    slot = fetch(step, blocks, [slots], sems)
    length = normed_ref.shape[0]
    width = slots.shape[2]
    for part in range(3):
        columns = pl.ds(part * width, width)
        found = mm(normed_ref[...], slots[slot, part], NT) + bias_ref[0, :, columns]
        projected_ref[0, :, columns] = found.astype(bf16)
    for pair in range(width // PAIR):
        base = pair * PAIR

        def read(part, rows, base=base):
            return projected_ref[0, rows, pl.ds(part * width + base, PAIR)]

        def write(rows, value, base=base):
            attended_ref[0, rows, pl.ds(base, PAIR)] = value

        attend_pair(read, write, log_ref.at[0, pair], length, min(512, length))
    found = mm(attended_ref[0], slots[slot, 3])

    @pl.when(step == 0)
    def _():
        merged_ref[...] = found

    @pl.when(step > 0)
    def _():
        merged_ref[...] += found


def still(shape):
    zeros = (0,) * len(shape)
    return pl.BlockSpec(shape, lambda k: zeros, pipeline_mode=pl.Buffered(buffer_count=1))


def moving(shape, offset=0):
    zeros = (0,) * (len(shape) - 1)
    return pl.BlockSpec((1,) + shape[1:], lambda k: (offset + k,) + zeros)


ANYWHERE = pl.BlockSpec(memory_space=pl.ANY)


def scalar(shape):
    return pl.BlockSpec(memory_space=pltpu.SMEM)


def slots_of(count, blocks):
    depth = min(2, count)
    return [pltpu.VMEM((depth,) + array.shape, bf16) for array in blocks[0]] + [
        pltpu.SemaphoreType.DMA((depth, len(blocks[0])))
    ]


def outs_of(count, lead, tensors, rows, depth):
    shape = (min(2, count), 2, lead, tensors, rows // (2 * tensors), depth)
    scratch = (min(2, count), lead, tensors, 2, rows // (2 * tensors), depth)
    return shape, [pltpu.VMEM(scratch, bf16), pltpu.SemaphoreType.DMA((min(2, count), lead, 2))]


def call(kernel, count, operands, outs, scratch, flops, exps):
    in_specs = [make(a.shape) if make is not None else ANYWHERE for make, a in operands]
    out_specs = [make(s) if make is not None else ANYWHERE for make, s, _ in outs]
    moved = sum(a.size * a.dtype.itemsize for _, a in operands)
    moved += sum(math.prod(s) * jnp.dtype(d).itemsize for _, s, d in outs)
    return pl.pallas_call(
        functools.partial(kernel, count=count),
        grid=(count,),
        in_specs=in_specs,
        out_specs=out_specs,
        out_shape=[jax.ShapeDtypeStruct(s, d) for _, s, d in outs],
        scratch_shapes=scratch,
        compiler_params=pltpu.CompilerParams(
            vmem_limit_bytes=VMEM_LIMIT, dimension_semantics=("arbitrary",)
        ),
        cost_estimate=pl.CostEstimate(
            flops=flops // COST_SHARE, bytes_accessed=moved // COST_SHARE, transcendentals=exps // COST_SHARE
        ),
    )(*[a for _, a in operands])


def attend_ahead(normed, bias, blocks):
    length, depth = normed.shape
    count, width = len(blocks), blocks[0][0].shape[1]
    return call(
        attend_ahead_kernel,
        count,
        [(still, normed), (moving, bias)] + [(None, array) for block in blocks for array in block],
        [
            (moving, (count, length, 3 * width), bf16),
            (moving, (count, length, width), bf16),
            (moving, (count, width // PAIR, 2, length), f32),
            (still, (length, depth), f32),
        ],
        slots_of(count, blocks),
        count * width * length * (8 * depth + 16 * length),
        count * width * length * length // HD,
    )


def attend_pair_back(read, write_query, dk_sum, dv_sum, log_ref, length, block):
    lane = lax.broadcasted_iota(jnp.int32, (1, PAIR), 1)
    keys = read(1, pl.ds(0, length))
    values = read(2, pl.ds(0, length))
    turned = jnp.transpose(keys)
    factor = log2_e * score_scale
    for start in range(0, length, block):
        rows = pl.ds(start, block)
        queries = read(0, rows)
        grads = read(4, rows)
        product = jnp.transpose(grads.astype(f32) * read(3, rows).astype(f32))
        query_grads = []
        key_part = None
        value_part = None
        for h in range(2):
            mine = (lane // HD) == h
            own_q = jnp.where(mine, queries, jnp.zeros_like(queries))
            own_g = jnp.where(mine, grads, jnp.zeros_like(grads))
            inner = jnp.sum(product[h * HD : (h + 1) * HD], axis=0, keepdims=True)
            scores = mm(keys, own_q, NT)
            prob = jnp.exp2(scores * factor - log_ref[h, rows][None])
            grad_prob = mm(values, own_g, NT)
            grad_scores = (prob * (grad_prob - inner)).astype(bf16)
            key_term = mm(grad_scores, own_q)
            value_term = mm(prob.astype(bf16), own_g)
            key_part = key_term if key_part is None else key_part + key_term
            value_part = value_term if value_part is None else value_part + value_term
            query_grads.append(mm(turned[h * HD : (h + 1) * HD], grad_scores))
        both = jnp.transpose(jnp.concatenate(query_grads, axis=0))
        write_query(rows, (both * score_scale).astype(bf16))
        if start == 0:
            dk_sum[...] = key_part
            dv_sum[...] = value_part
        else:
            dk_sum[...] += key_part
            dv_sum[...] += value_part


def attend_back_kernel(*refs, count):
    place_ref, grad_ref, normed_ref, projected_ref, attended_ref, log_ref = refs[:6]
    blocks = [refs[6 + j : 7 + j] for j in range(count)]
    out_refs, refs = refs[6 + count : -10], refs[-10:]
    sums_ref, total_ref, slots, sems, outs, out_sems, inward, parts, dk_sum, dv_sum = refs
    step = pl.program_id(0)
    place = place_ref[0]
    slot = fetch(step, blocks, [slots], sems)
    out = slot_free(step, count, outs, out_refs, out_sems, place)
    length = normed_ref.shape[0]
    width = slots.shape[2]
    inward[...] = mm(grad_ref[...], slots[slot, 3], NT).astype(bf16)
    for pair in range(width // PAIR):
        base = pair * PAIR

        def read(part, rows, base=base):
            if part == 3:
                return attended_ref[0, rows, pl.ds(base, PAIR)]
            if part == 4:
                return inward[rows, pl.ds(base, PAIR)]
            return projected_ref[0, rows, pl.ds(part * width + base, PAIR)]

        def write_query(rows, value, base=base):
            parts[rows, pl.ds(base, PAIR)] = value

        attend_pair_back(
            read, write_query, dk_sum, dv_sum, log_ref.at[0, pair], length, min(256, length)
        )
        parts[:, pl.ds(width + base, PAIR)] = (dk_sum[...] * score_scale).astype(bf16)
        parts[:, pl.ds(2 * width + base, PAIR)] = dv_sum[...].astype(bf16)
    found = None
    for part in range(3):
        columns = pl.ds(part * width, width)
        outs[out, part] = mm(parts[:, columns], normed_ref[...], TN).astype(bf16).reshape(outs.shape[2:])
        sums_ref[0, :, columns] = jnp.sum(parts[:, columns].astype(f32), axis=0, keepdims=True)
        term = mm(parts[:, columns], slots[slot, part])
        found = term if found is None else found + term
    outs[out, 3] = mm(attended_ref[0], grad_ref[...], TN).astype(bf16).reshape(outs.shape[2:])
    hand_out(step, count, outs, out_refs, out_sems, place)

    @pl.when(step == 0)
    def _():
        total_ref[...] = found

    @pl.when(step > 0)
    def _():
        total_ref[...] += found


def attend_back(place, tensors, grad_merged, normed, projected, attended, logs, blocks, offset):
    length, depth = normed.shape
    count, width = len(blocks), blocks[0][0].shape[1]
    at = functools.partial(moving, offset=offset)
    shape, outs = outs_of(count, 4, tensors, width, depth)
    results = call(
        attend_back_kernel,
        count,
        [(scalar, place), (still, grad_merged), (still, normed)]
        + [(at, projected), (at, attended), (at, logs)]
        + [(None, array) for block in blocks for array in block],
        [(None, shape, bf16)] * max(1, count // 2)
        + [(moving, (count, 1, 3 * width), f32), (still, (length, depth), f32)],
        slots_of(count, blocks)
        + outs
        + [
            pltpu.VMEM((length, width), bf16),
            pltpu.VMEM((length, 3 * width), bf16),
            pltpu.VMEM((length, PAIR), f32),
            pltpu.VMEM((length, PAIR), f32),
        ],
        count * width * length * (16 * depth + 32 * length),
        count * width * length * length // HD,
    )
    return results[:-2], results[-2], results[-1]


def feed_ahead_kernel(*refs, count):
    normed_ref, bias_ref = refs[:2]
    blocks = [refs[2 + 2 * j : 4 + 2 * j] for j in range(count)]
    act_ref, slope_ref, total_ref, expand, shrink, sems = refs[2 + 2 * count :]
    step = pl.program_id(0)
    slot = fetch(step, blocks, [expand, shrink], sems)
    length = normed_ref.shape[0]
    block = min(256, length)
    bias = bias_ref[0]
    for start in range(0, length, block):
        rows = pl.ds(start, block)
        before = mm(normed_ref[rows, :], expand[slot], NT) + bias
        phi = 0.5 * (1.0 + lax.erf(before * inv_root_two))
        act_ref[0, rows, :] = (before * phi).astype(bf16)
        bell = jnp.exp2(before * before * (-0.5 * log2_e)) * inv_root_tau
        slope_ref[0, rows, :] = (phi + before * bell).astype(bf16)
    found = mm(act_ref[0], shrink[slot])

    @pl.when(step == 0)
    def _():
        total_ref[...] = found

    @pl.when(step > 0)
    def _():
        total_ref[...] += found


def feed_ahead(normed, bias, blocks):
    length, depth = normed.shape
    count, hidden = len(blocks), blocks[0][0].shape[0]
    return call(
        feed_ahead_kernel,
        count,
        [(still, normed), (moving, bias)] + [(None, array) for block in blocks for array in block],
        [
            (moving, (count, length, hidden), bf16),
            (moving, (count, length, hidden), bf16),
            (still, (length, depth), f32),
        ],
        slots_of(count, blocks),
        4 * count * hidden * length * depth,
        2 * count * hidden * length,
    )


def feed_back_kernel(*refs, count):
    place_ref, grad_ref, normed_ref, act_ref, slope_ref = refs[:5]
    blocks = [refs[5 + 2 * j : 7 + 2 * j] for j in range(count)]
    out_refs, refs = refs[5 + 2 * count : -8], refs[-8:]
    sums_ref, total_ref, expand, shrink, sems, outs, out_sems, inward = refs
    step = pl.program_id(0)
    place = place_ref[0]
    slot = fetch(step, blocks, [expand, shrink], sems)
    out = slot_free(step, count, outs, out_refs, out_sems, place)
    length = normed_ref.shape[0]
    block = min(256, length)
    outs[out, 1] = mm(act_ref[0], grad_ref[...], TN).astype(bf16).reshape(outs.shape[2:])
    summed = None
    for start in range(0, length, block):
        rows = pl.ds(start, block)
        before = mm(grad_ref[rows, :], shrink[slot], NT) * slope_ref[0, rows, :].astype(f32)
        before = before.astype(bf16)
        inward[rows, :] = before
        part = jnp.sum(before.astype(f32), axis=0, keepdims=True)
        summed = part if summed is None else summed + part
    sums_ref[0] = summed
    outs[out, 0] = mm(inward[...], normed_ref[...], TN).astype(bf16).reshape(outs.shape[2:])
    hand_out(step, count, outs, out_refs, out_sems, place)
    found = mm(inward[...], expand[slot])

    @pl.when(step == 0)
    def _():
        total_ref[...] = found

    @pl.when(step > 0)
    def _():
        total_ref[...] += found


def feed_back(place, tensors, grad_shrunk, normed, activated, slope, blocks, offset):
    length, depth = normed.shape
    count, hidden = len(blocks), blocks[0][0].shape[0]
    at = functools.partial(moving, offset=offset)
    shape, outs = outs_of(count, 2, tensors, hidden, depth)
    results = call(
        feed_back_kernel,
        count,
        [(scalar, place), (still, grad_shrunk), (still, normed), (at, activated), (at, slope)]
        + [(None, array) for block in blocks for array in block],
        [(None, shape, bf16)] * max(1, count // 2)
        + [(moving, (count, 1, hidden), f32), (still, (length, depth), f32)],
        slots_of(count, blocks) + outs + [pltpu.VMEM((length, hidden), bf16)],
        8 * count * hidden * length * depth,
        0,
    )
    return results[:-2], results[-2], results[-1]


def swapped(value, axis, bits):
    count = lax.axis_size(axis)
    flat = value.reshape(-1, value.shape[-1])
    flat = lax.ppermute(flat, axis, [(i, i ^ bits) for i in range(count)])
    return flat.reshape(value.shape)


def is_first():
    return lax.axis_index(SECTION) == 0


def tie(*values):
    return lax.optimization_barrier(values)


def spread(value, axis):
    whole = value[None]
    for bit in (1 << i for i in range(lax.axis_size(axis).bit_length() - 1)):
        other = swapped(whole, axis, bit)
        low = (lax.axis_index(axis) & bit) == 0
        whole = jnp.concatenate([jnp.where(low, whole, other), jnp.where(low, other, whole)])
    return whole


def own_part(shard, axis, split):
    if not split:
        return shard
    size = shard.shape[axis] // lax.axis_size(DP)
    return lax.dynamic_slice_in_dim(shard, lax.axis_index(DP) * size, size, axis)


def exchanged(values):
    return lax.all_to_all(values, TENSOR, 0, 0, tiled=True)


def plus(a, b):
    return (a.astype(f32) + b.astype(f32)).astype(bf16)


class Scatter:
    def __init__(self, layer):
        self.layer = layer

    def start(self, odd, even):
        self.even = even
        self.got = swapped(odd, DP, 1)
        self.stage = self.one

    def one(self, got):
        half = self.even.shape[2] // 2
        keep = plus(self.even[:, 0, :half], got[:, 0, :half])
        send = plus(self.even[:, 1, :half], got[:, 1, :half])
        stay = plus(self.even[0, :, half:], got[0, :, half:])
        leave = plus(self.even[1, :, half:], got[1, :, half:])
        return (keep, stay, send, leave)

    def after_one(self, outs):
        self.keep, self.stay, send, leave = outs
        self.got = (swapped(send, SECTION, 1), swapped(leave, DP, 2))
        self.stage = self.two

    def two(self, got):
        mine, leave = plus(self.keep[0], got[0][0]), plus(self.keep[1], got[0][1])
        return (mine, plus(self.stay[0], got[1][0]), leave, plus(self.stay[1], got[1][1]))

    def after_two(self, outs):
        self.mine, self.stay, leave, send = outs
        self.got = (swapped(leave, DP, 2), swapped(send, SECTION, 1))
        self.stage = self.three

    def three(self, got):
        whole = jnp.concatenate([plus(self.mine, got[0]), plus(self.stay, got[1])])
        lead, tensors, rows, depth = whole.shape
        return jnp.transpose(whole, (1, 0, 2, 3)).reshape(tensors, lead * rows, depth)

    def after_three(self, whole):
        lead = 2 * self.mine.shape[0]
        piece = lax.psum_scatter(whole, TENSOR, scatter_dimension=0, tiled=True)
        self.got = piece.reshape(lead, -1, whole.shape[-1])
        self.stage = self.four

    def four(self, got):
        return got

    def after_four(self, piece):
        self.piece = piece
        self.got = lax.ppermute(piece, SECTION, [(1 - self.layer, self.layer)])
        self.stage = self.end

    def end(self, got):
        first = is_first()
        low = jnp.where(first, self.piece, got)
        return jnp.concatenate([low, jnp.where(first, got, self.piece)], axis=1)

    def after_end(self, shard):
        self.shard = shard

    def whole_sum(self, block):
        whole = lax.psum(block, DP)
        piece = lax.psum_scatter(whole, TENSOR, scatter_dimension=2, tiled=True)[:, :, 0]
        first = is_first()
        piece = jnp.stack([jnp.where(first, piece[0], piece[1]), jnp.where(first, piece[1], piece[0])])
        piece = plus(piece, lax.ppermute(piece, SECTION, [(1 - self.layer, self.layer)]))
        self.shard = jnp.concatenate([piece[0], piece[1]], axis=1)


class Join:
    def __init__(self, piece):
        self.piece = piece
        self.got = swapped(piece, DP, 2)
        self.stage = self.far

    def far(self, got):
        low = (lax.axis_index(DP) & 2) == 0
        return jnp.stack([jnp.where(low, self.piece, got), jnp.where(low, got, self.piece)])

    def after_far(self, pair):
        self.pair = pair
        self.got = swapped(pair, DP, 1)
        self.stage = self.near

    def near(self, got):
        low = (lax.axis_index(DP) & 1) == 0
        even, odd = jnp.where(low, self.pair, got), jnp.where(low, got, self.pair)
        return [even[0], odd[0], even[1], odd[1]]

    def after_near(self, parts):
        self.parts = parts


class Return:
    def __init__(self, layer, grad, tensors):
        self.layer = layer
        self.got = exchanged(grad.reshape(tensors, -1, grad.shape[1]))
        self.stage = self.over

    def over(self, got):
        return got

    def after_over(self, cut):
        self.cut = cut
        self.other = lax.ppermute(cut, SECTION, [(1 - self.layer, self.layer)])


class Total:
    def __init__(self, value):
        self.bits = [
            (axis, 1 << i)
            for axis in (DP, TENSOR, SECTION)
            for i in range(lax.axis_size(axis).bit_length() - 1)
        ]
        self.send(value)

    def send(self, value):
        self.value = value
        self.stage = self.add if self.bits else None
        if self.bits:
            self.got = swapped(value, *self.bits.pop(0))

    def add(self, got):
        return self.value + got

    def after_add(self, value):
        self.send(value)


def advance(chain, *jobs):
    got, chain = tie([job.got for job in jobs], chain)
    stages = [job.stage for job in jobs]
    outs = [stage(value) for stage, value in zip(stages, got)]
    outs, chain = tie(outs, chain)
    for job, stage, out in zip(jobs, stages, outs):
        getattr(job, "after_" + stage.__name__)(out)
    return chain


def normalize_parts(resid):
    centre = resid - jnp.mean(resid, axis=-1, keepdims=True)
    spread = jnp.mean(centre * centre, axis=-1, keepdims=True)
    inverse = lax.rsqrt(spread + epsilon)
    return (centre * inverse, inverse)


def normalize_back(grad_scaled, scaled, inverse):
    mean_grad = jnp.mean(grad_scaled, axis=-1, keepdims=True)
    mean_cross = jnp.mean(grad_scaled * scaled, axis=-1, keepdims=True)
    return inverse * (grad_scaled - mean_grad - scaled * mean_cross)


def block_order(blocks):
    return sorted(blocks, key=lambda k: (k + 1) % 2)


def in_groups(blocks, count):
    order = block_order(blocks)
    size = len(order) // min(count, len(order))
    return [(start, order[start : start + size]) for start in range(0, len(order), size)]


def attend_half(rows, vectors, blocks):
    resid = rows.astype(f32)
    scaled_one, _ = normalize_parts(resid)
    normed_one = (scaled_one * vectors[ATTEND_GAIN] + vectors[ATTEND_SHIFT]).astype(bf16)
    order = block_order(blocks)
    bias = jnp.stack([vectors[TRIPLE_BIAS][k] for k in order])[:, None]
    projected, attended, logs, merged = attend_ahead(normed_one, bias, [blocks[k] for k in order])
    return (normed_one, projected, attended, logs, merged)


def feed_half(rows, merged, vectors, blocks):
    merged = merged + vectors[MERGE_BIAS]
    middle = rows.astype(f32) + vectors[ATTEND_SCALE] * merged
    scaled_two, _ = normalize_parts(middle)
    normed_two = (scaled_two * vectors[FEED_GAIN] + vectors[FEED_SHIFT]).astype(bf16)
    order = block_order(blocks)
    bias = jnp.stack([vectors[EXPAND_BIAS][k] for k in order])[:, None]
    activated, slope, shrunk = feed_ahead(normed_two, bias, [blocks[k] for k in order])
    shrunk = shrunk + vectors[SHRINK_BIAS]
    result = (middle + vectors[FEED_SCALE] * shrunk).astype(bf16)
    return (result, merged, normed_two, activated, slope, shrunk)


def layer_back(place, tensors, grad_output, saved, vectors, attend_blocks, feed_blocks, sums, hooks):
    rows, normed_one, projected, attended, logs, merged, normed_two, activated, slope, shrunk = saved
    grads = {}
    grad_wide = grad_output.astype(f32)
    grad_shrunk = (vectors[FEED_SCALE] * grad_wide).astype(bf16)
    grads[FEED_SCALE] = jnp.sum(grad_wide * shrunk, axis=0)
    grads[SHRINK_BIAS] = jnp.sum(grad_shrunk.astype(f32), axis=0)

    order = block_order(feed_blocks)
    parts, columns, product = feed_back(
        place, tensors, grad_shrunk, normed_two, activated, slope, [feed_blocks[k] for k in order], 0
    )
    grads[EXPAND_BIAS] = {k: columns[i] for i, k in enumerate(order)}
    product, parts = hooks[KERNEL]((product, parts))
    sums[FEED].start(*parts)

    resid = rows.astype(f32)
    middle = resid + vectors[ATTEND_SCALE] * merged
    scaled_one, inverse_one = normalize_parts(resid)
    scaled_two, inverse_two = normalize_parts(middle)
    grads[FEED_GAIN] = jnp.sum(product * scaled_two, axis=0)
    grads[FEED_SHIFT] = jnp.sum(product, axis=0)
    grad_middle = grad_wide + normalize_back(product * vectors[FEED_GAIN], scaled_two, inverse_two)
    grad_merged = (vectors[ATTEND_SCALE] * grad_middle).astype(bf16)
    grads[ATTEND_SCALE] = jnp.sum(grad_middle * merged, axis=0)
    grads[MERGE_BIAS] = jnp.sum(grad_merged.astype(f32), axis=0)
    grad_merged = hooks[FEED](grad_merged)

    total = None
    grads[TRIPLE_BIAS] = {}
    parts = []
    groups = in_groups(attend_blocks, hooks[GROUPS])
    for i, (offset, ks) in enumerate(groups):
        found_parts, columns, found = attend_back(
            place, tensors, grad_merged, normed_one, projected, attended, logs,
            [attend_blocks[k] for k in ks], offset,
        )
        for j, k in enumerate(ks):
            cut = columns[j].reshape(3, -1)
            grads[TRIPLE_BIAS][k] = jnp.stack([cut[0], cut[2]])
        parts.extend(found_parts)
        if i == 0 and len(groups) == 2:
            parts, grad_merged, found = hooks[MIDWAY]((parts, grad_merged, found))
            sums[ATTEND].start(parts[0], None)
        total = found if total is None else total + found
    if len(parts) == 1:
        sums[ATTEND].whole_sum(parts[0][0])
        total = hooks[ATTEND](total)
    elif len(groups) == 2:
        sums[ATTEND].even = parts[1]
        total = hooks[ATTEND](total)
    else:
        total, parts = hooks[ATTEND]((total, parts))
        sums[ATTEND].start(*parts)
    grads[ATTEND_GAIN] = jnp.sum(total * scaled_one, axis=0)
    grads[ATTEND_SHIFT] = jnp.sum(total, axis=0)
    grad_input = grad_middle + normalize_back(total * vectors[ATTEND_GAIN], scaled_one, inverse_one)
    return (hooks[END](grad_input.astype(bf16)), grads)


def body(
    boundary,
    counts,
    attend_gain,
    attend_shift,
    triple_weight,
    triple_bias,
    merge_weight,
    merge_bias,
    attend_scale,
    feed_gain,
    feed_shift,
    expand_weight,
    expand_bias,
    shrink_weight,
    shrink_bias,
    feed_scale,
):
    sections, tensors, replicas = (lax.axis_size(axis) for axis in EVERY)
    section, tensor, replica = (lax.axis_index(axis) for axis in EVERY)
    first = section == 0
    members = sections * tensors
    _, micro, slots, share, depth = boundary.shape
    images = micro * slots
    assert images <= members and sections == 2 and replicas == 4
    heads_split = (triple_bias.shape[2] // HD) % replicas == 0

    biases = spread(jnp.concatenate([triple_bias[0].reshape(-1), expand_bias[0]]), TENSOR)
    names = (
        ATTEND_GAIN,
        ATTEND_SHIFT,
        MERGE_BIAS,
        ATTEND_SCALE,
        FEED_GAIN,
        FEED_SHIFT,
        SHRINK_BIAS,
        FEED_SCALE,
    )
    plain = (
        attend_gain,
        attend_shift,
        merge_bias,
        attend_scale,
        feed_gain,
        feed_shift,
        shrink_bias,
        feed_scale,
    )
    small = spread(jnp.concatenate([value[0] for value in plain] + [biases.reshape(-1)]), SECTION)

    attend_piece = jnp.concatenate(
        [
            jnp.transpose(own_part(triple_weight[0], 2, heads_split), (1, 2, 0)),
            own_part(merge_weight[0], 0, heads_split)[None],
        ]
    )
    expand_piece = jnp.transpose(own_part(expand_weight[0], 1, True))
    shrink_piece = own_part(shrink_weight[0], 0, True)

    spread_rows = boundary[0].reshape(images, share, depth)
    spread_rows = jnp.pad(spread_rows, ((0, members - images), (0, 0), (0, 0)))
    near, far = spread_rows[:tensors], spread_rows[tensors:]
    leaving = jnp.where(first, far, near)

    home = lax.all_gather(attend_piece, TENSOR, axis=1, tiled=True)
    other_expand = swapped(expand_piece, SECTION, 1)
    leaving, other_expand = tie(leaving, other_expand)
    passed = swapped(leaving, SECTION, 1)

    def whole(layer, own, other):
        return lax.all_gather(jnp.where(section == layer, own, other), TENSOR, axis=0, tiled=True)

    expand_own = [whole(0, expand_piece, other_expand)]
    home, passed, shrink_piece, small = tie(home, passed, shrink_piece, small)
    rows = exchanged(jnp.where(first, near, passed))
    foreign = swapped(home, SECTION, 1)
    beyond = swapped(home, DP, 2) if heads_split else home
    other_shrink = swapped(shrink_piece, SECTION, 1)
    rows, beyond, foreign, other_shrink, expand_own[0], shrink_piece, expand_piece = tie(
        rows, beyond, foreign, other_shrink, expand_own[0], shrink_piece, expand_piece
    )
    foreign_beyond = swapped(beyond, SECTION, 1) if heads_split else foreign
    shrink_own = [whole(0, shrink_piece, other_shrink)]
    expand_own.append(whole(1, expand_piece, other_expand))
    shrink_own.append(whole(1, shrink_piece, other_shrink))

    def around(value):
        return {0: value, 1: swapped(value, DP, 1), 2: swapped(value, DP, 2)}

    expand_next = around(expand_own[0])
    rows, foreign_beyond, expand_next = tie(rows, foreign_beyond, expand_next)
    rows = rows.reshape(tensors * share, depth)
    cotangent = jnp.where(first, passed, far)
    mine = section * tensors + tensor
    at = jnp.minimum(mine, images - 1)
    held = lax.dynamic_index_in_dim(counts[:, 0], at // slots, 0, keepdims=False)
    live = jnp.logical_and(mine < images, at % slots < held)

    def both(home, foreign):
        return jnp.where(first, home, foreign), jnp.where(first, foreign, home)

    attend_blocks = [{}, {}]
    for k, pair in ((0, both(home, foreign)), (2, both(beyond, foreign_beyond)))[: 2 if heads_split else 1]:
        for layer in range(sections):
            attend_blocks[layer][k] = (pair[layer],)
            if heads_split:
                attend_blocks[layer][k + 1] = (swapped(pair[layer], DP, 1),)

    def full(blocks):
        return {**blocks, 3: swapped(blocks[2], DP, 1)}

    def paired(expand, shrink):
        return {k: (expand[k], shrink[k]) for k in expand}

    def block_part(value, axis, which):
        size = value.shape[axis] // replicas
        return lax.dynamic_slice_in_dim(value, jnp.bitwise_xor(replica, which) * size, size, axis)

    vectors = []
    for layer in range(sections):
        named = {name: small[layer, i * depth : (i + 1) * depth] for i, name in enumerate(names)}
        by_tensor = small[layer, len(names) * depth :].reshape(tensors, -1)
        width = triple_bias.shape[2]
        query, value, hidden = (
            by_tensor[:, :width],
            by_tensor[:, width : 2 * width],
            by_tensor[:, 2 * width :],
        )
        named[TRIPLE_BIAS] = {}
        for k in attend_blocks[layer]:
            q_part, v_part = query, value
            if heads_split:
                q_part, v_part = block_part(query, 1, k), block_part(value, 1, k)
            q_part, v_part = q_part.reshape(-1), v_part.reshape(-1)
            named[TRIPLE_BIAS][k] = jnp.concatenate([q_part, jnp.zeros_like(q_part), v_part])
        named[EXPAND_BIAS] = {k: block_part(hidden, 1, k).reshape(-1) for k in range(replicas)}
        vectors.append(named)

    shrink_own[0], rows = tie(shrink_own[0], rows)
    shrink_next = around(shrink_own[0])
    normed, projected, attended, logs, merged = attend_half(rows, vectors[0], attend_blocks[0])
    shrink_next, attend_blocks[1], expand_own[1], merged = tie(
        shrink_next, attend_blocks[1], expand_own[1], merged
    )
    blocks = paired(full(expand_next), full(shrink_next))
    expand_next = around(expand_own[1])
    result, merged, normed_two, activated, slope, shrunk = feed_half(rows, merged, vectors[0], blocks)
    feed_blocks = [blocks]
    kept = [(rows, normed, projected, attended, logs, merged, normed_two, activated, slope, shrunk)]
    expand_next, shrink_own[1], cotangent, rows = tie(expand_next, shrink_own[1], cotangent, result)
    shrink_next = around(shrink_own[1])
    cotangent = exchanged(cotangent)
    normed, projected, attended, logs, merged = attend_half(rows, vectors[1], attend_blocks[1])
    shrink_next, cotangent, merged = tie(shrink_next, cotangent, merged)
    blocks = paired(full(expand_next), full(shrink_next))
    _, merged, normed_two, activated, slope, shrunk = feed_half(rows, merged, vectors[1], blocks)
    feed_blocks.append(blocks)
    kept.append((rows, normed, projected, attended, logs, merged, normed_two, activated, slope, shrunk))
    cotangent = cotangent.reshape(tensors * share, depth)
    cotangent = jnp.where(live, cotangent, jnp.zeros_like(cotangent))

    def whole_of(blocks):
        rows_of = blocks[0].shape[0]
        cuts = jnp.stack([blocks[k].reshape(rows_of, tensors, -1) for k in sorted(blocks)], axis=2)
        if len(blocks) == 1:
            return cuts.reshape(-1)
        order = jnp.bitwise_xor(replica, jnp.arange(replicas))
        return jnp.take(cuts, order, axis=2).reshape(-1)

    place = section.astype(jnp.int32).reshape(1)
    sums = [{ATTEND: Scatter(layer), FEED: Scatter(layer)} for layer in range(sections)]
    feed, attend = [found[FEED] for found in sums], [found[ATTEND] for found in sums]
    attend_jobs = (lambda layer: [attend[layer]]) if heads_split else (lambda layer: [])
    extra = {}

    def packed(layer):
        found = vector_grads[layer]
        return jnp.concatenate(
            [found[name] for name in names]
            + [whole_of(found[TRIPLE_BIAS]), whole_of(found[EXPAND_BIAS])]
        )

    def after_second(grad):
        grad = advance(grad, *attend_jobs(1))
        extra[1] = Return(1, grad, tensors)
        return grad

    hooks = {
        GROUPS: 1,
        KERNEL: lambda chain: chain,
        FEED: lambda chain: advance(chain, feed[1]),
        ATTEND: lambda chain: advance(chain, feed[1]),
        END: after_second,
    }
    vector_grads = [None] * sections
    grad, vector_grads[1] = layer_back(
        place, tensors, cotangent, kept[1], vectors[1], attend_blocks[1], feed_blocks[1], sums[1], hooks
    )
    extra[TOTAL] = Total(packed(1))

    def midway(chain):
        return advance(chain, feed[0], feed[1], extra[TOTAL], *attend_jobs(1))

    def after_first(grad):
        extra[0] = Return(0, grad, tensors)
        return grad

    hooks = {
        GROUPS: 2,
        KERNEL: lambda chain: advance(chain, feed[1], extra[1], extra[TOTAL], *attend_jobs(1)),
        FEED: lambda chain: advance(chain, feed[0], extra[TOTAL]),
        MIDWAY: midway,
        ATTEND: lambda chain: advance(
            chain, feed[0], feed[1], extra[TOTAL], *attend_jobs(0), *attend_jobs(1)
        ),
        END: after_first,
    }
    if not heads_split:
        hooks[ATTEND] = lambda chain: advance(midway(chain), feed[0], feed[1], extra[TOTAL])
    chain, vector_grads[0] = layer_back(
        place, tensors, grad, kept[0], vectors[0], attend_blocks[0], feed_blocks[0], sums[0], hooks
    )
    last = Total(packed(0))
    chain = advance(chain, last, *attend_jobs(0))
    chain = advance(chain, last, *attend_jobs(0))
    chain = advance(chain, feed[0])
    chain = advance(chain, extra[0], feed[0], last, extra[TOTAL], *attend_jobs(1))
    while extra[TOTAL].stage is not None:
        chain = advance(chain, extra[TOTAL])
    feed_join = Join(jnp.where(first, feed[0].shard, feed[1].shard))
    if heads_split:
        chain = advance(chain, feed_join, attend[0])
        chain = advance(chain, feed_join, attend[0], last)
        attend_join = Join(jnp.where(first, attend[0].shard, attend[1].shard))
        chain = advance(chain, attend_join)
        chain = advance(chain, last, attend_join)
        attend_parts = attend_join.parts
    else:
        chain = advance(advance(chain, feed_join, last), feed_join, last)
        attend_parts = [jnp.where(first, attend[0].shard, attend[1].shard)]
        while last.stage is not None:
            chain = advance(chain, last)
    near = jnp.where(first, extra[0].cut, extra[1].other)
    far = jnp.where(first, extra[0].other, extra[1].cut)
    boundary_grad = jnp.concatenate([near, far])[:images].reshape(1, micro, slots, share, depth)
    total = jnp.where(first, last.value, extra[TOTAL].value)

    triple_grad = jnp.concatenate([part[:3] for part in attend_parts], axis=1)
    triple_grad = jnp.transpose(triple_grad.astype(f32), (2, 0, 1))
    merge_grad = jnp.concatenate([part[3] for part in attend_parts]).astype(f32)
    expand_grad = jnp.concatenate([part[0] for part in feed_join.parts])
    expand_grad = jnp.transpose(expand_grad.astype(f32))
    shrink_grad = jnp.concatenate([part[1] for part in feed_join.parts]).astype(f32)

    named = {name: total[i * depth : (i + 1) * depth] for i, name in enumerate(names)}
    rest = total[len(names) * depth :]
    bias_width, hidden_width = triple_bias.shape[2], expand_bias.shape[1]
    pair = rest[: 2 * tensors * bias_width].reshape(2, -1)
    triple_bias_grad = lax.dynamic_slice_in_dim(pair, tensor * bias_width, bias_width, 1)
    expand_bias_grad = lax.dynamic_slice_in_dim(
        rest[2 * tensors * bias_width :], tensor * hidden_width, hidden_width
    )
    return (
        boundary_grad,
        named[ATTEND_GAIN][None],
        named[ATTEND_SHIFT][None],
        triple_grad[None],
        triple_bias_grad[None],
        merge_grad[None],
        named[MERGE_BIAS][None],
        named[ATTEND_SCALE][None],
        named[FEED_GAIN][None],
        named[FEED_SHIFT][None],
        expand_grad[None],
        expand_bias_grad[None],
        shrink_grad[None],
        named[SHRINK_BIAS][None],
        named[FEED_SCALE][None],
    )


def solution(mesh):
    placed = (
        P(SECTION, None, DP, TENSOR, None),
        P(None, DP),
        P(SECTION, None),
        P(SECTION, None),
        P(SECTION, None, None, TENSOR),
        P(SECTION, None, TENSOR),
        P(SECTION, TENSOR, None),
        P(SECTION, None),
        P(SECTION, None),
        P(SECTION, None),
        P(SECTION, None),
        P(SECTION, None, TENSOR),
        P(SECTION, TENSOR),
        P(SECTION, TENSOR, None),
        P(SECTION, None),
        P(SECTION, None),
    )
    return jax.shard_map(
        body,
        mesh=mesh,
        in_specs=placed,
        out_specs=placed[:1] + placed[2:],
        check_vma=False,
    )
```
